128 devices in a mesh: grp: 2 (over y_lo), dap: 64 (over z, x, y_hi, core).
Axes of the slice: x: 4, y: 4 (y_hi: 2, y_lo: 2; y = y_hi * 2 + y_lo), z: 4, core: 2. Of those that a mesh axis runs over, the one named last changes fastest.
Arguments:
- homolog_matrix: bfloat16 [512, 512, 256], P(('grp', 'dap')), may hold values from -6 to 6
- pair_state: bfloat16 [512, 512, 128], P('dap', 'grp'), may hold values from -6 to 6
- alignment_entry_mask: int32 [512, 512], P(('grp', 'dap')), may hold values 0 or 1
- residue_chain_index: int32 [512], replicated, may hold values from 0 to 3, as said below
- horizontal_scale_vector: float32 [256], replicated, may hold values from 0.1 to 1.9
- pair_norm_gain: float32 [128], replicated, may hold values from 0.1 to 1.9
- pair_bias_weight: bfloat16 [8, 128], replicated, may hold values from -15 to 15
- interchain_bias: float32 [8], replicated, may hold values from -2 to 2
- horizontal_query_projector: bfloat16 [256, 1024], replicated, may hold values from -0.375 to 0.375
- horizontal_final_projector: bfloat16 [256, 256], replicated, may hold values from -0.375 to 0.375
- vertical_scale_vector: float32 [256], replicated, may hold values from 0.1 to 1.9
- column_input_weight: bfloat16 [256, 1024], replicated, may hold values from -7 to 7
- vertical_final_projector: bfloat16 [256, 256], replicated, may hold values from -0.375 to 0.375
- feedforward_scale_vector: float32 [256], replicated, may hold values from 0.1 to 1.9
- feedforward_expand_matrix: bfloat16 [256, 1024], replicated, may hold values from -0.375 to 0.375
- feedforward_shrink_matrix: bfloat16 [1024, 256], replicated, may hold values from -0.1875 to 0.1875
Outputs:
- msa_out: bfloat16 [512, 512, 256], P(('grp', 'dap'))
The draws below stay inside these ranges and needn't reach their ends.
Inputs may be any that keep to these rules, and one draw needn't show every extreme that they name: residue_chain_index never falls along the residues; each of the four chains is one run of residues.
All inputs are finite; a program needn't handle non-finite values. No bound on the sum of `alignment_entry_mask` on one device may be relied on, other than what follows from the above.
Results may differ from the reference program's by a relative error of at most 0.0095.
The reference program's roundings to bfloat16 on the way count: a program that leaves them out, or rounds other values in their place, can miss the bound.
Values may be sent and summed in bfloat16 or wider, within the bound.
No kernel may reach another device: no remote copies, remote signals or barrier semaphores. Data moves between devices by JAX's collectives and lax.ppermute only.
A program may use at most 128 MiB of HBM per device.

```python
import jax
import jax.numpy as jnp
from jax import lax

FEATURE_SIZE = 256
CZ = 128
H = 8
HIDDEN_UNITS = 1024
HOMOLOG_TOTAL = 512
AMINO_TOTAL = 512


def draw_residue_chain_index(key, part):
    key = jax.random.fold_in(key, 5)
    reach = AMINO_TOTAL // 16
    offsets = jax.random.randint(key, (3,), -reach, reach + 1)
    cuts = jnp.arange(1, 4, dtype=jnp.int32) * AMINO_TOTAL // 4 + offsets
    position = jnp.arange(AMINO_TOTAL, dtype=jnp.int32)
    return jnp.sum((position[:, None] >= cuts[None, :]).astype(jnp.int32), axis=1).astype(jnp.int32)


def draw_pair_bias_weight(key, part):
    key = jax.random.fold_in(key, 11)
    entries = jnp.clip(jax.random.normal(key, (H, CZ), jnp.float32), -4.0, 4.0) * CZ ** (-0.5)
    return entries.astype(jnp.bfloat16)


def draw_column_input_weight(key, part):
    key = jax.random.fold_in(key, 17)
    entries = jnp.clip(jax.random.normal(key, (FEATURE_SIZE, 4 * FEATURE_SIZE), jnp.float32), -4.0, 4.0) * FEATURE_SIZE ** (-0.5)
    return entries.astype(jnp.bfloat16)


def touch_ends(result, key, low, high):
    shape = result.shape
    place = [jax.random.randint(jax.random.fold_in(key, axis), (), 0, shape[axis]) for axis in range(len(shape))]
    result = result.at[tuple(place)].set(low)
    longest = shape.index(max(shape))
    place[longest] = (place[longest] + 1) % shape[longest]
    return result.at[tuple(place)].set(high)


def shard_levels(own_key, shape, pieces, smallest, top_value):
    loudness = 1.0
    for axis_at, parts in pieces:
        draws = jax.random.uniform(jax.random.fold_in(jax.random.fold_in(own_key, 6), axis_at), (parts,), jnp.float32, smallest / len(pieces), top_value / len(pieces))
        loudness = loudness * jnp.repeat(jnp.exp(draws), shape[axis_at] // parts).reshape((-1,) + (1,) * (len(shape) - 1 - axis_at))
    return loudness


def bell_draw(rng, dims, width, most, shards=(), kind=jnp.bfloat16):
    values = width * jax.random.normal(rng, dims, jnp.float32)
    if shards:
        values = values * shard_levels(rng, dims, shards, -0.22, 0.18)
    return jnp.clip(values, -most, most).astype(kind)


def setup_inputs(seed: int = 0) -> dict:
    streams_of = jax.random.split(jax.random.key(seed), 17)
    homolog_matrix = bell_draw(streams_of[0], (HOMOLOG_TOTAL, AMINO_TOTAL, FEATURE_SIZE), 1.0, 6.0, ((0, 128),))
    pair_state = bell_draw(streams_of[1], (AMINO_TOTAL, AMINO_TOTAL, CZ), 1.0, 6.0, ((0, 64), (1, 2)))
    alignment_entry_mask = touch_ends((jax.random.randint(streams_of[2], (HOMOLOG_TOTAL, AMINO_TOTAL), 0, 8) < 7).astype(jnp.int32), jax.random.fold_in(streams_of[2], 1), 0, 1)
    residue_chain_index = draw_residue_chain_index(jax.random.fold_in(streams_of[16], 71), 0)
    horizontal_scale_vector = jnp.clip(1.0 + 0.18 * jax.random.normal(streams_of[4], (FEATURE_SIZE,), jnp.float32), 0.1, 1.9)
    pair_norm_gain = jnp.clip(1.0 + 0.18 * jax.random.normal(streams_of[5], (CZ,), jnp.float32), 0.1, 1.9)
    pair_bias_weight = draw_pair_bias_weight(jax.random.fold_in(streams_of[16], 71), 0)
    interchain_bias = jnp.clip(jax.random.uniform(streams_of[7], (H,), jnp.float32, -2.0, 2.0), -2.0, 2.0)
    horizontal_query_projector = bell_draw(streams_of[8], (FEATURE_SIZE, 4 * FEATURE_SIZE), FEATURE_SIZE ** -0.5, 0.375)
    horizontal_final_projector = bell_draw(streams_of[9], (FEATURE_SIZE, FEATURE_SIZE), FEATURE_SIZE ** -0.5, 0.375)
    vertical_scale_vector = jnp.clip(1.0 + 0.18 * jax.random.normal(streams_of[10], (FEATURE_SIZE,), jnp.float32), 0.1, 1.9)
    column_input_weight = draw_column_input_weight(jax.random.fold_in(streams_of[16], 71), 0)
    vertical_final_projector = bell_draw(streams_of[12], (FEATURE_SIZE, FEATURE_SIZE), FEATURE_SIZE ** -0.5, 0.375)
    feedforward_scale_vector = jnp.clip(1.0 + 0.18 * jax.random.normal(streams_of[13], (FEATURE_SIZE,), jnp.float32), 0.1, 1.9)
    feedforward_expand_matrix = bell_draw(streams_of[14], (FEATURE_SIZE, HIDDEN_UNITS), FEATURE_SIZE ** -0.5, 0.375)
    feedforward_shrink_matrix = bell_draw(streams_of[15], (HIDDEN_UNITS, FEATURE_SIZE), HIDDEN_UNITS ** -0.5, 0.1875)
    return {"homolog_matrix": homolog_matrix, "pair_state": pair_state, "alignment_entry_mask": alignment_entry_mask, "residue_chain_index": residue_chain_index, "horizontal_scale_vector": horizontal_scale_vector, "pair_norm_gain": pair_norm_gain, "pair_bias_weight": pair_bias_weight, "interchain_bias": interchain_bias, "horizontal_query_projector": horizontal_query_projector, "horizontal_final_projector": horizontal_final_projector, "vertical_scale_vector": vertical_scale_vector, "column_input_weight": column_input_weight, "vertical_final_projector": vertical_final_projector, "feedforward_scale_vector": feedforward_scale_vector, "feedforward_expand_matrix": feedforward_expand_matrix, "feedforward_shrink_matrix": feedforward_shrink_matrix}


EPSILON = 1e-05
NEGATIVE_FILL = 1000000000.0

def layer_norm_apply(field, gain):
    field = field.astype(jnp.float32)
    average = lax.optimization_barrier(jnp.mean(field, axis=-1, keepdims=True))
    center = field - average
    spread = lax.optimization_barrier(jnp.mean(center * center, axis=-1, keepdims=True))
    return center * lax.rsqrt(spread + EPSILON) * gain

def rounded_length(field):
    return lax.optimization_barrier(field.astype(jnp.bfloat16))

def softmax_rows(scores):
    highest = lax.optimization_barrier(jnp.max(scores, axis=-1, keepdims=True))
    powers = jnp.exp(scores - highest)
    return powers / lax.optimization_barrier(jnp.sum(powers, axis=-1, keepdims=True))

def gated_attention(normed, proj_weight, out_weight, bias_term, key_mask_term, head_count):
    length = normed.shape[0]
    channel_width = out_weight.shape[0]
    head_size = channel_width // head_count
    packed = rounded_length(jnp.dot(normed, proj_weight, preferred_element_type=jnp.float32)).astype(jnp.float32)
    queries = packed[:, :channel_width].reshape(length, head_count, head_size)
    keys_all = packed[:, channel_width:2 * channel_width].reshape(length, head_count, head_size)
    attended_vectors = packed[:, 2 * channel_width:3 * channel_width].reshape(length, head_count, head_size)
    gates = packed[:, 3 * channel_width:]
    scores = jnp.einsum('qhd,khd->hqk', queries, keys_all) * head_size ** (-0.5)
    scores = scores + bias_term + key_mask_term[None, None, :]
    weights = rounded_length(softmax_rows(scores)).astype(jnp.float32)
    blended = jnp.einsum('hqk,khd->qhd', weights, attended_vectors).reshape(length, channel_width)
    gated = rounded_length(blended * jax.nn.sigmoid(gates))
    return jnp.dot(gated, out_weight, preferred_element_type=jnp.float32)

def reference(homolog_matrix, pair_state, alignment_entry_mask, residue_chain_index, horizontal_scale_vector, pair_norm_gain, pair_bias_weight, interchain_bias, horizontal_query_projector, horizontal_final_projector, vertical_scale_vector, column_input_weight, vertical_final_projector, feedforward_scale_vector, feedforward_expand_matrix, feedforward_shrink_matrix):
    head_count = pair_bias_weight.shape[0]
    pair_normed = rounded_length(layer_norm_apply(pair_state, pair_norm_gain)).astype(jnp.float32)
    pair_bias = jnp.einsum('ijc,hc->hij', pair_normed, pair_bias_weight.astype(jnp.float32))
    cross_pairs = (residue_chain_index[:, None] != residue_chain_index[None, :]).astype(jnp.float32)
    pair_bias = pair_bias + interchain_bias[:, None, None] * cross_pairs[None]
    pair_bias = rounded_length(pair_bias).astype(jnp.float32)
    key_mask_term = (alignment_entry_mask.astype(jnp.float32) - 1.0) * NEGATIVE_FILL

    def single_row_attention(inputs):
        sequence, mask_row = inputs
        normed = rounded_length(layer_norm_apply(sequence, horizontal_scale_vector))
        return gated_attention(normed, horizontal_query_projector, horizontal_final_projector, pair_bias, mask_row, head_count)
    row_update_terms = lax.map(single_row_attention, (homolog_matrix, key_mask_term))
    alignment_after_rows = (homolog_matrix.astype(jnp.float32) + row_update_terms).astype(jnp.bfloat16)

    def single_column_attention(inputs):
        vertical_gated_softmax, mask_col = inputs
        normed = rounded_length(layer_norm_apply(vertical_gated_softmax, vertical_scale_vector))
        column_update_term = gated_attention(normed, column_input_weight, vertical_final_projector, 0.0, mask_col, head_count)
        alignment_after_columns = (vertical_gated_softmax.astype(jnp.float32) + column_update_term).astype(jnp.bfloat16)
        transition_input_normed = rounded_length(layer_norm_apply(alignment_after_columns, feedforward_scale_vector))
        hidden = rounded_length(jax.nn.relu(jnp.dot(transition_input_normed, feedforward_expand_matrix, preferred_element_type=jnp.float32)))
        residual_update = jnp.dot(hidden, feedforward_shrink_matrix, preferred_element_type=jnp.float32)
        return (alignment_after_columns.astype(jnp.float32) + residual_update).astype(jnp.bfloat16)
    completed_alignment = lax.map(single_column_attention, (jnp.swapaxes(alignment_after_rows, 0, 1), jnp.swapaxes(key_mask_term, 0, 1)))
    return jnp.swapaxes(completed_alignment, 0, 1)
```

```python
import functools
import math

import jax
import jax.numpy as jnp
import ml_dtypes
import numpy as np
from jax import lax
from jax.experimental import pallas as pl
from jax.experimental.pallas import tpu as pltpu
from jax.sharding import Mesh, PartitionSpec as P

EPSILON = 1e-05
HEADS = 8
HEAD = 32
WIDTH = 256
LENGTH = 512
HALF = 256
PEERS = 64
TILE_ROWS = 72
LOG2E = math.log2(math.e)
SCALE = HEAD**-0.5 * LOG2E
F32 = jnp.float32
BF16 = jnp.bfloat16
AXES = ("grp", "z", "x", "yh", "core")
PLANE = ("grp", "z", "x", "yh")
VMEM_LIMIT = 50 * 1024 * 1024

MASK_TERM = 1e9 * HEAD**0.5


def mask_parts():
    parts = []
    rest = MASK_TERM
    for _ in range(3):
        part = float(np.asarray(rest, ml_dtypes.bfloat16))
        parts.append(part)
        rest -= part
    return parts


def nt(a, b):
    return lax.dot_general(a, b, (((1,), (1,)), ((), ())), preferred_element_type=F32)


def tn(a, b):
    return lax.dot_general(a, b, (((0,), (0,)), ((), ())), preferred_element_type=F32)


def nn(a, b):
    return jnp.dot(a, b, preferred_element_type=F32)


def norm(x, gain):
    average = jnp.mean(x, axis=-1, keepdims=True)
    center = x - average
    spread = jnp.mean(center * center, axis=-1, keepdims=True)
    return (center * lax.rsqrt(spread + EPSILON) * gain).astype(BF16)


def position():
    q = (lax.axis_index("z") * 4 + lax.axis_index("x")) * 2 + lax.axis_index("yh")
    return lax.axis_index("grp"), q, lax.axis_index("core")


def bias_kernel(pair_ref, gain_ref, weight_ref, chain_s_ref, chain_v_ref, inter_ref, out_ref):
    grp, q, core = position()
    normed = norm(pair_ref[...].astype(F32), gain_ref[...])
    bias = nt(weight_ref[...], normed)
    chain_cols = chain_v_ref[pl.ds(grp, 1), :]
    inter = inter_ref[...]
    parts = []
    for ii in range(8):
        chain_row = chain_s_ref[16 * q + 8 * core + ii]
        cross = (chain_cols != chain_row).astype(F32)
        parts.append(bias[:, ii * 256 : (ii + 1) * 256] + inter * cross)
    stacked = jnp.stack(parts, axis=0)
    out_ref[...] = jnp.swapaxes(stacked, 0, 1).reshape(64, 256).astype(BF16)


def payload_kernel(bias_ref, own_ref, other_ref, out_ref):
    _, _, core = position()
    own = own_ref[...].astype(F32)
    other = other_ref[...].astype(F32)
    first = jnp.where(core == 0, own, other)
    second = jnp.where(core == 0, other, own)
    mask = jnp.concatenate([first, second], axis=0).astype(BF16)
    i = lax.broadcasted_iota(jnp.int32, (LENGTH, HALF), 0)
    l = lax.broadcasted_iota(jnp.int32, (LENGTH, HALF), 1)
    pick = (i == (l // 8) * 16 + core * 8 + l % 8).astype(F32).astype(BF16)
    rows = nn(mask, pick).astype(BF16)
    tile = jnp.concatenate([bias_ref[...].astype(F32), rows.astype(F32)], axis=0).astype(BF16)

    def put(p, carry):
        out_ref[p] = tile
        return carry

    lax.fori_loop(0, PEERS, put, 0)


def project_kernel(
    own_ref, other_ref, mask_ref, gain_ref, wk_ref, wt_ref, k_ref, vt_ref, qt_ref, gt_ref, xq_ref
):
    step = pl.program_id(0)
    _, _, core = position()
    x = jnp.where(step < 4, own_ref[0].astype(F32), other_ref[0].astype(F32))
    normed = norm(x, gain_ref[...])
    k_ref[0, :, :WIDTH] = nn(normed, wk_ref[...]).astype(BF16)
    lane = lax.broadcasted_iota(jnp.int32, (8, 128), 1)
    row = lax.broadcasted_iota(jnp.int32, (8, 128), 0)
    consts = mask_parts()
    pick = jnp.zeros((8, 128), F32)
    for at, value in enumerate(consts):
        pick = jnp.where((lane == at) & (row == step), value, pick)
    k_ref[0, :, WIDTH:] = nn(mask_ref[...] - 1, pick.astype(BF16)).astype(BF16)
    vt_ref[0] = nt(wt_ref[2 * WIDTH : 3 * WIDTH], normed).astype(BF16)

    def half(a):
        rows = a.reshape(32, 2, 8, WIDTH)
        return jnp.where(core == 0, rows[:, 0], rows[:, 1]).reshape(HALF, WIDTH)

    xq = half(x)
    xq_ref[0] = xq.astype(BF16)
    normed_q = half(normed.astype(F32)).astype(BF16)
    qt_ref[0] = nt(wt_ref[:WIDTH], normed_q).astype(BF16)
    gt_ref[0] = nt(wt_ref[3 * WIDTH :], normed_q).astype(BF16)


def attend(keys, mask_tile, vt, qt, bias, queries):
    ones_rows = jnp.ones((128, queries), BF16)
    ones_v = jnp.ones((16, LENGTH), BF16)
    augmented = [
        jnp.concatenate([keys[:, g * 128 : (g + 1) * 128], mask_tile], axis=1) for g in range(2)
    ]
    out = []
    for h in range(HEADS):
        group, at = divmod(h, 4)
        pieces = []
        if at:
            pieces.append(jnp.zeros((HEAD * at, queries), BF16))
        pieces.append(qt[h * HEAD : (h + 1) * HEAD])
        if at < 3:
            pieces.append(jnp.zeros((HEAD * (3 - at), queries), BF16))
        pieces.append(ones_rows)
        spread = jnp.concatenate(pieces, axis=0)
        scores = nn(augmented[group], spread) * SCALE
        if bias is not None:
            scores = scores + bias[h]
        highest = jnp.max(scores, axis=0, keepdims=True)
        powers = jnp.exp2(scores - highest).astype(BF16)
        values = jnp.concatenate([vt[h * HEAD : (h + 1) * HEAD], ones_v], axis=0)
        blended = nn(values, powers)
        out.append(blended[:HEAD] / blended[HEAD : HEAD + 1])
    return jnp.concatenate(out, axis=0)


def row_kernel(tile_ref, k_ref, vt_ref, qt_ref, gt_ref, xq_ref, wo_ref, out_ref, bias_ref, y_ref):
    step = pl.program_id(0)
    _, _, core = position()

    @pl.when(step == 0)
    def _():
        row = lax.broadcasted_iota(jnp.int32, (HALF, HALF), 0)
        col = lax.broadcasted_iota(jnp.int32, (HALF, HALF), 1)
        eye = (row == col).astype(F32).astype(BF16)
        for g in range(2):
            for pair in range(4):
                block = tile_ref[g * 32 : (g + 1) * 32, pair * 16 : (pair + 1) * 16, :]
                block = block.astype(F32).reshape(32, 2, 8, 256)
                for k in range(2):
                    rows = block[:, k].reshape(HALF, 256).astype(BF16)
                    bias_ref[pair * 2 + k, g * 256 : (g + 1) * 256, :] = nt(eye, rows) * LOG2E

    o = attend(k_ref[0, :, :WIDTH], k_ref[0, :, WIDTH:], vt_ref[0], qt_ref[0], bias_ref, HALF)
    gated = (o * jax.nn.sigmoid(gt_ref[0].astype(F32))).astype(BF16)
    y = xq_ref[0].astype(F32) + tn(gated, wo_ref[...])
    s = lax.rem(step + 4 * core, 8)
    for j in range(2):
        y_ref[j, pl.ds(s, HALF, stride=8), :] = y[:, j * 128 : (j + 1) * 128]

    @pl.when(step == 7)
    def _():
        for j in range(2):
            out_ref[:, j * 128 : (j + 1) * 128] = y_ref[j].astype(BF16)


def column_kernel(
    x_ref, mask_ref, gain_ref, wk_ref, wt_ref, wo_ref, gain2_ref, w1_ref, w2_ref, out_ref,
    x32_ref, y_ref,
):
    r = pl.program_id(0)
    grp, q, _ = position()
    peer = grp * 32 + q

    @pl.when(r == 0)
    def _():
        x32_ref[...] = x_ref[...].astype(F32).reshape(PEERS, 4, 8, WIDTH)

    x = x32_ref[:, r].reshape(LENGTH, WIDTH)
    normed = norm(x, gain_ref[...])
    keys = nn(normed, wk_ref[...]).astype(BF16)
    lane = lax.broadcasted_iota(jnp.int32, (HALF, 128), 1)
    row = lax.broadcasted_iota(jnp.int32, (HALF, 128), 0)
    pick = jnp.zeros((HALF, 128), F32)
    for at, value in enumerate(mask_parts()):
        pick = jnp.where((lane == at) & (row == 4 * peer + r), value, pick)
    mask_tile = nn(mask_ref[...] - 1, pick.astype(BF16)).astype(BF16)
    vt = nt(wt_ref[2 * WIDTH : 3 * WIDTH], normed).astype(BF16)
    qt = nt(wt_ref[:WIDTH], normed).astype(BF16)
    gt = nt(wt_ref[3 * WIDTH :], normed).astype(BF16)
    for part in range(2):
        cols = slice(part * HALF, (part + 1) * HALF)
        o = attend(keys, mask_tile, vt, qt[:, cols], None, HALF)
        gated = (o * jax.nn.sigmoid(gt[:, cols].astype(F32))).astype(BF16)
        one = x[cols] + tn(gated, wo_ref[...])
        two = one.astype(BF16).astype(F32)
        hidden = jnp.maximum(nn(norm(two, gain2_ref[...]), w1_ref[...]), 0.0).astype(BF16)
        y = two + nn(hidden, w2_ref[...])
        for j in range(2):
            y_ref[j, pl.ds(part * 4 * HALF + r, HALF, stride=4), :] = y[:, j * 128 : (j + 1) * 128]

    @pl.when(r == 3)
    def _():
        for j in range(2):
            out_ref[:, j * 128 : (j + 1) * 128] = y_ref[j].astype(BF16)


def whole(*shape):
    return pl.BlockSpec(shape, lambda i: (0,) * len(shape))


def each(*shape):
    return pl.BlockSpec((1,) + shape, lambda i: (i,) + (0,) * len(shape))


def body(
    homolog,
    pair_state,
    mask,
    chain,
    row_gain,
    pair_gain,
    pair_weight,
    interchain,
    row_in,
    row_out,
    col_gain,
    col_in,
    col_out,
    ff_gain,
    ff_expand,
    ff_shrink,
):
    params = pltpu.CompilerParams(vmem_limit_bytes=VMEM_LIMIT)
    swap = [(0, 1), (1, 0)]
    other_mask = lax.ppermute(mask, "core", swap)
    other = lax.ppermute(homolog, "core", swap)

    bias = pl.pallas_call(
        bias_kernel,
        out_shape=jax.ShapeDtypeStruct((64, 256), BF16),
        in_specs=[
            pl.BlockSpec(memory_space=pltpu.VMEM),
            pl.BlockSpec(memory_space=pltpu.VMEM),
            pl.BlockSpec(memory_space=pltpu.VMEM),
            pl.BlockSpec(memory_space=pltpu.SMEM),
            pl.BlockSpec(memory_space=pltpu.VMEM),
            pl.BlockSpec(memory_space=pltpu.VMEM),
        ],
        compiler_params=params,
    )(
        pair_state.reshape(2048, 128),
        pair_gain.reshape(1, 128),
        pair_weight,
        chain,
        chain.reshape(2, 256),
        interchain.reshape(8, 1),
    )
    payload = pl.pallas_call(
        payload_kernel,
        out_shape=jax.ShapeDtypeStruct((PEERS, TILE_ROWS, 256), BF16),
        compiler_params=params,
    )(bias, mask, other_mask)
    tiles = lax.all_to_all(payload, PLANE, 0, 0, tiled=True)

    row_in_t = row_in.T
    col_in_t = col_in.T
    mask_t = jnp.concatenate([mask, other_mask], axis=0).astype(BF16).T
    keys, vt, qt, gt, xq = pl.pallas_call(
        project_kernel,
        grid=(8,),
        out_shape=[
            jax.ShapeDtypeStruct((8, LENGTH, WIDTH + 128), BF16),
            jax.ShapeDtypeStruct((8, WIDTH, LENGTH), BF16),
            jax.ShapeDtypeStruct((8, WIDTH, HALF), BF16),
            jax.ShapeDtypeStruct((8, WIDTH, HALF), BF16),
            jax.ShapeDtypeStruct((8, HALF, WIDTH), BF16),
        ],
        in_specs=[
            pl.BlockSpec((1, LENGTH, WIDTH), lambda i: (jnp.minimum(i, 3), 0, 0)),
            pl.BlockSpec((1, LENGTH, WIDTH), lambda i: (jnp.maximum(i - 4, 0), 0, 0)),
            whole(LENGTH, 8),
            whole(1, WIDTH),
            whole(WIDTH, WIDTH),
            whole(4 * WIDTH, WIDTH),
        ],
        out_specs=[
            each(LENGTH, WIDTH + 128),
            each(WIDTH, LENGTH),
            each(WIDTH, HALF),
            each(WIDTH, HALF),
            each(HALF, WIDTH),
        ],
        compiler_params=params,
        cost_estimate=pl.CostEstimate(
            flops=2 * 8 * 512 * 256 * 768, bytes_accessed=9 * 2**20, transcendentals=0
        ),
    )(
        homolog,
        other,
        mask_t,
        row_gain.reshape(1, WIDTH),
        row_in[:, WIDTH : 2 * WIDTH],
        row_in_t,
    )

    after_rows = pl.pallas_call(
        row_kernel,
        grid=(8,),
        out_shape=jax.ShapeDtypeStruct((8 * HALF, WIDTH), BF16),
        in_specs=[
            whole(PEERS, TILE_ROWS, 256),
            each(LENGTH, WIDTH + 128),
            each(WIDTH, LENGTH),
            each(WIDTH, HALF),
            each(WIDTH, HALF),
            each(HALF, WIDTH),
            whole(WIDTH, WIDTH),
        ],
        out_specs=whole(8 * HALF, WIDTH),
        scratch_shapes=[
            pltpu.VMEM((HEADS, LENGTH, HALF), F32),
            pltpu.VMEM((2, 8 * HALF, 128), F32),
        ],
        compiler_params=params,
        cost_estimate=pl.CostEstimate(
            flops=2 * 8 * 8 * 512 * 256 * 512, bytes_accessed=9 * 2**20, transcendentals=8 * 2**20
        ),
    )(tiles, keys, vt, qt, gt, xq, row_out)

    columns = lax.all_to_all(after_rows.reshape(PEERS, 32, WIDTH), PLANE, 0, 0, tiled=True)
    col_mask = tiles[:, 64:, :].reshape(LENGTH, HALF)

    finished = pl.pallas_call(
        column_kernel,
        grid=(4,),
        out_shape=jax.ShapeDtypeStruct((4 * LENGTH, WIDTH), BF16),
        in_specs=[
            whole(PEERS, 32, WIDTH),
            whole(LENGTH, HALF),
            whole(1, WIDTH),
            whole(WIDTH, WIDTH),
            whole(4 * WIDTH, WIDTH),
            whole(WIDTH, WIDTH),
            whole(1, WIDTH),
            whole(WIDTH, 4 * WIDTH),
            whole(4 * WIDTH, WIDTH),
        ],
        out_specs=whole(4 * LENGTH, WIDTH),
        scratch_shapes=[
            pltpu.VMEM((PEERS, 4, 8, WIDTH), F32),
            pltpu.VMEM((2, 4 * LENGTH, 128), F32),
        ],
        compiler_params=params,
        cost_estimate=pl.CostEstimate(
            flops=2 * 8 * 8 * 512 * 256 * 512, bytes_accessed=4 * 2**20, transcendentals=8 * 2**20
        ),
    )(
        columns,
        col_mask,
        col_gain.reshape(1, WIDTH),
        col_in[:, WIDTH : 2 * WIDTH],
        col_in_t,
        col_out,
        ff_gain.reshape(1, WIDTH),
        ff_expand,
        ff_shrink,
    )

    back = lax.all_to_all(finished.reshape(128, 16, WIDTH), AXES, 0, 0, tiled=True)
    back = back.reshape(32, 2, 2, 4, 4, WIDTH)
    return jnp.transpose(back, (3, 0, 2, 1, 4, 5)).reshape(4, LENGTH, WIDTH)


def solution(mesh):
    inner = Mesh(mesh.devices.reshape(2, 4, 4, 2, 2), AXES)
    dap = ("z", "x", "yh", "core")
    return jax.shard_map(
        body,
        mesh=inner,
        in_specs=(P(AXES, None, None), P(dap, "grp", None), P(AXES, None)) + (P(),) * 13,
        out_specs=P(AXES, None, None),
        check_vma=False,
    )
```

```python
import functools
import math

import jax
import jax.numpy as jnp
import ml_dtypes
import numpy as np
from jax import lax
from jax.experimental import pallas as pl
from jax.experimental.pallas import tpu as pltpu
from jax.sharding import Mesh, PartitionSpec as P

EPSILON = 1e-05
HEADS = 8
HEAD = 32
WIDTH = 256
LENGTH = 512
HALF = 256
PEERS = 64
BATCH = 2
LOG2E = math.log2(math.e)
SCALE = HEAD**-0.5 * LOG2E
F32 = jnp.float32
BF16 = jnp.bfloat16
AXES = ("grp", "z", "x", "yh", "core")
PLANE = ("grp", "z", "x", "yh")
VMEM_LIMIT = 50 * 1024 * 1024

MASK_TERM = 1e9 * HEAD**0.5


def mask_parts():
    parts = []
    rest = MASK_TERM
    for _ in range(3):
        part = float(np.asarray(rest, ml_dtypes.bfloat16))
        parts.append(part)
        rest -= part
    return parts


def nt(a, b):
    return lax.dot_general(a, b, (((1,), (1,)), ((), ())), preferred_element_type=F32)


def tn(a, b):
    return lax.dot_general(a, b, (((0,), (0,)), ((), ())), preferred_element_type=F32)


def nn(a, b):
    return jnp.dot(a, b, preferred_element_type=F32)


def norm(x, gain):
    average = jnp.mean(x, axis=-1, keepdims=True)
    center = x - average
    spread = jnp.mean(center * center, axis=-1, keepdims=True)
    return (center * lax.rsqrt(spread + EPSILON) * gain).astype(BF16)


def position():
    q = (lax.axis_index("z") * 4 + lax.axis_index("x")) * 2 + lax.axis_index("yh")
    return lax.axis_index("grp"), q, lax.axis_index("core")


def bias_kernel(pair_ref, gain_ref, weight_ref, chain_ref, inter_ref, out_ref):
    grp, q, core = position()
    normed = norm(pair_ref[...].astype(F32), gain_ref[...])
    bias = nt(weight_ref[...], normed)
    chain = chain_ref[...]
    cols = jnp.where(grp == 0, chain[:, :256], chain[:, 256:])
    place = lax.broadcasted_iota(jnp.int32, (8, LENGTH), 1)
    wanted = 16 * q + 8 * core + lax.broadcasted_iota(jnp.int32, (8, LENGTH), 0)
    rows = jnp.sum(jnp.where(place == wanted, chain, 0), axis=1, keepdims=True)
    cross = (rows != cols).astype(F32)
    row = lax.broadcasted_iota(jnp.int32, (8, 8), 0)
    col = lax.broadcasted_iota(jnp.int32, (8, 8), 1)
    inter = jnp.sum(jnp.where(row == col, inter_ref[...], 0.0), axis=1, keepdims=True)
    parts = [
        bias[:, ii * 256 : (ii + 1) * 256] + inter * cross[ii : ii + 1] for ii in range(8)
    ]
    stacked = jnp.stack(parts, axis=0)
    tile = jnp.swapaxes(stacked, 0, 1).reshape(64, 256).astype(BF16)

    def put(p, carry):
        out_ref[p] = tile
        return carry

    lax.fori_loop(0, PEERS, put, 0)


def project_kernel(
    own_ref, other_ref, mask_ref, own_mask_ref, other_mask_ref, gain_ref, wk_ref, wt_ref,
    k_ref, vt_ref, qt_ref, gt_ref, xq_ref, mask_out_ref,
):
    step = pl.program_id(0)
    _, _, core = position()
    x = jnp.where(step < 4, own_ref[0].astype(F32), other_ref[0].astype(F32))
    normed = norm(x, gain_ref[...])
    k_ref[0, :, :WIDTH] = nn(normed, wk_ref[...]).astype(BF16)
    lane = lax.broadcasted_iota(jnp.int32, (8, 128), 1)
    row = lax.broadcasted_iota(jnp.int32, (8, 128), 0)
    consts = mask_parts()
    pick = jnp.zeros((8, 128), F32)
    for at, value in enumerate(consts):
        pick = jnp.where((lane == at) & (row == step), value, pick)
    k_ref[0, :, WIDTH:] = nn(mask_ref[...] - 1, pick.astype(BF16)).astype(BF16)
    vt_ref[0] = nt(wt_ref[2 * WIDTH : 3 * WIDTH], normed).astype(BF16)

    def half(a):
        rows = a.reshape(32, 2, 8, WIDTH)
        return jnp.where(core == 0, rows[:, 0], rows[:, 1]).reshape(HALF, WIDTH)

    xq = half(x)
    xq_ref[0] = xq.astype(BF16)
    normed_q = half(normed.astype(F32)).astype(BF16)
    qt_ref[0] = nt(wt_ref[:WIDTH], normed_q).astype(BF16)
    gt_ref[0] = nt(wt_ref[3 * WIDTH :], normed_q).astype(BF16)

    @pl.when(step == 0)
    def _():
        own = own_mask_ref[...].astype(F32)
        other = other_mask_ref[...].astype(F32)
        first = jnp.where(core == 0, own, other)
        second = jnp.where(core == 0, other, own)
        mask = jnp.concatenate([first, second], axis=0).astype(BF16)
        i = lax.broadcasted_iota(jnp.int32, (LENGTH, HALF), 0)
        l = lax.broadcasted_iota(jnp.int32, (LENGTH, HALF), 1)
        pick = (i == (l // 8) * 16 + core * 8 + l % 8).astype(F32).astype(BF16)
        mask_out_ref[...] = nn(mask, pick).astype(BF16)


def spread(qt, h, mask_rows):
    at = h % 4
    queries = qt.shape[1]
    pieces = []
    if at:
        pieces.append(jnp.zeros((HEAD * at, queries), BF16))
    pieces.append(qt[h * HEAD : (h + 1) * HEAD])
    if at < 3:
        pieces.append(jnp.zeros((HEAD * (3 - at), queries), BF16))
    pieces.append(mask_rows)
    return jnp.concatenate(pieces, axis=0)


def attend(parts, bias):
    mask_rows = jnp.ones((128, HALF), BF16)
    ones_v = jnp.ones((16, LENGTH), BF16)
    augmented = [
        [jnp.concatenate([keys[:, g * 128 : (g + 1) * 128], tile], axis=1) for g in range(2)]
        for keys, tile, _, _ in parts
    ]
    units = [(part, h) for part in range(len(parts)) for h in range(HEADS)]

    def score(part, h):
        return nn(augmented[part][h // 4], spread(parts[part][3], h, mask_rows))

    def blend(part, h, powers):
        vt = parts[part][2]
        values = jnp.concatenate([vt[h * HEAD : (h + 1) * HEAD], ones_v], axis=0)
        blended = nn(values, powers)
        return blended[:HEAD] / blended[HEAD : HEAD + 1]

    out = []
    scores = score(*units[0])
    powers = None
    for at, (part, h) in enumerate(units):
        later = score(*units[at + 1]) if at + 1 < len(units) else None
        scaled = scores * SCALE
        if bias is not None:
            scaled = scaled + bias[h]
        highest = jnp.max(scaled, axis=0, keepdims=True)
        now = jnp.exp2(scaled - highest).astype(BF16)
        if at:
            out.append(blend(*units[at - 1], powers))
        powers = now
        scores = later
    out.append(blend(*units[-1], powers))
    return [
        jnp.concatenate(out[part * HEADS : (part + 1) * HEADS], axis=0)
        for part in range(len(parts))
    ]


def row_kernel(
    tile_ref, k_ref, vt_ref, qt_ref, gt_ref, xq_ref, wo_ref, mask_ref, out_ref, bias_ref, y_ref
):
    step = pl.program_id(0)
    _, _, core = position()

    @pl.when(step == 0)
    def _():
        row = lax.broadcasted_iota(jnp.int32, (HALF, HALF), 0)
        col = lax.broadcasted_iota(jnp.int32, (HALF, HALF), 1)
        eye = (row == col).astype(F32).astype(BF16)
        for g in range(2):
            for pair in range(4):
                block = tile_ref[g * 32 : (g + 1) * 32, pair * 16 : (pair + 1) * 16, :]
                block = block.astype(F32).reshape(32, 2, 8, 256)
                for k in range(2):
                    rows = block[:, k].reshape(HALF, 256).astype(BF16)
                    bias_ref[pair * 2 + k, g * 256 : (g + 1) * 256, :] = nt(eye, rows) * LOG2E

    parts = [
        (k_ref[n, :, :WIDTH], k_ref[n, :, WIDTH:], vt_ref[n], qt_ref[n]) for n in range(BATCH)
    ]
    for n, o in enumerate(attend(parts, bias_ref)):
        gated = (o * jax.nn.sigmoid(gt_ref[n].astype(F32))).astype(BF16)
        y = xq_ref[n].astype(F32) + tn(gated, wo_ref[...])
        s = lax.rem(step * BATCH + n + 4 * core, 8)
        for j in range(2):
            y_ref[j, pl.ds(s, HALF, stride=8), :] = y[:, j * 128 : (j + 1) * 128]

    @pl.when(step == 8 // BATCH - 1)
    def _():
        for j in range(2):
            lanes = slice(j * 128, (j + 1) * 128)
            out_ref[:, :32, lanes] = y_ref[j].astype(BF16).reshape(PEERS, 32, 128)
        out_ref[:, 32:, :] = jnp.broadcast_to(mask_ref[...][None], (PEERS, 8, WIDTH))


def column_kernel(
    x_ref, gain_ref, wk_ref, wt_ref, wo_ref, gain2_ref, w1_ref, w2_ref, out_ref, x32_ref, y_ref
):
    r = pl.program_id(0)
    grp, q, _ = position()
    peer = grp * 32 + q

    @pl.when(r == 0)
    def _():
        x32_ref[...] = x_ref[...].astype(F32).reshape(PEERS, 5, 8, WIDTH)

    x = x32_ref[:, r].reshape(LENGTH, WIDTH)
    normed = norm(x, gain_ref[...])
    keys = nn(normed, wk_ref[...]).astype(BF16)
    lane = lax.broadcasted_iota(jnp.int32, (HALF, 128), 1)
    row = lax.broadcasted_iota(jnp.int32, (HALF, 128), 0)
    pick = jnp.zeros((HALF, 128), F32)
    for at, value in enumerate(mask_parts()):
        pick = jnp.where((lane == at) & (row == 4 * peer + r), value, pick)
    mask_tile = nn((x32_ref[:, 4].reshape(LENGTH, HALF) - 1.0).astype(BF16), pick.astype(BF16)).astype(BF16)
    vt = nt(wt_ref[2 * WIDTH : 3 * WIDTH], normed).astype(BF16)
    qt = nt(wt_ref[:WIDTH], normed).astype(BF16)
    gt = nt(wt_ref[3 * WIDTH :], normed).astype(BF16)
    parts = [(keys, mask_tile, vt, qt[:, n * HALF : (n + 1) * HALF]) for n in range(2)]
    for n, o in enumerate(attend(parts, None)):
        cols = slice(n * HALF, (n + 1) * HALF)
        gated = (o * jax.nn.sigmoid(gt[:, cols].astype(F32))).astype(BF16)
        one = x[cols] + tn(gated, wo_ref[...])
        two = one.astype(BF16).astype(F32)
        hidden = jnp.maximum(nn(norm(two, gain2_ref[...]), w1_ref[...]), 0.0).astype(BF16)
        y = two + nn(hidden, w2_ref[...])
        for j in range(2):
            y_ref[j, pl.ds(n * 4 * HALF + r, HALF, stride=4), :] = y[:, j * 128 : (j + 1) * 128]

    @pl.when(r == 3)
    def _():
        for j in range(2):
            out_ref[:, j * 128 : (j + 1) * 128] = y_ref[j].astype(BF16)


def whole(*shape):
    return pl.BlockSpec(shape, lambda i: (0,) * len(shape))


def each(count, *shape):
    return pl.BlockSpec((count,) + shape, lambda i: (i,) + (0,) * len(shape))


def body(
    homolog,
    pair_state,
    mask,
    chain,
    row_gain,
    pair_gain,
    pair_weight,
    interchain,
    row_in,
    row_out,
    col_gain,
    col_in,
    col_out,
    ff_gain,
    ff_expand,
    ff_shrink,
):
    params = pltpu.CompilerParams(vmem_limit_bytes=VMEM_LIMIT)
    swap = [(0, 1), (1, 0)]
    other_mask = lax.ppermute(mask, "core", swap)
    other = lax.ppermute(homolog, "core", swap)

    payload = pl.pallas_call(
        bias_kernel,
        grid=(1,),
        out_shape=jax.ShapeDtypeStruct((PEERS, 64, 256), BF16),
        in_specs=[whole(2048, 128), whole(1, 128), whole(8, 128), whole(1, LENGTH), whole(1, 8)],
        out_specs=whole(PEERS, 64, 256),
        compiler_params=params,
    )(
        pair_state.reshape(2048, 128),
        pair_gain.reshape(1, 128),
        pair_weight,
        chain.reshape(1, LENGTH),
        interchain.reshape(1, 8),
    )
    tiles = lax.all_to_all(payload, PLANE, 0, 0, tiled=True)

    row_in_t = row_in.T
    col_in_t = col_in.T
    mask_t = jnp.concatenate([mask, other_mask], axis=0).astype(BF16).T
    keys, vt, qt, gt, xq, mask_half = pl.pallas_call(
        project_kernel,
        grid=(8,),
        out_shape=[
            jax.ShapeDtypeStruct((8, LENGTH, WIDTH + 128), BF16),
            jax.ShapeDtypeStruct((8, WIDTH, LENGTH), BF16),
            jax.ShapeDtypeStruct((8, WIDTH, HALF), BF16),
            jax.ShapeDtypeStruct((8, WIDTH, HALF), BF16),
            jax.ShapeDtypeStruct((8, HALF, WIDTH), BF16),
            jax.ShapeDtypeStruct((8, HALF), BF16),
        ],
        in_specs=[
            pl.BlockSpec((1, LENGTH, WIDTH), lambda i: (jnp.minimum(i, 3), 0, 0)),
            pl.BlockSpec((1, LENGTH, WIDTH), lambda i: (jnp.maximum(i - 4, 0), 0, 0)),
            whole(LENGTH, 8),
            whole(4, LENGTH),
            whole(4, LENGTH),
            whole(1, WIDTH),
            whole(WIDTH, WIDTH),
            whole(4 * WIDTH, WIDTH),
        ],
        out_specs=[
            each(1, LENGTH, WIDTH + 128),
            each(1, WIDTH, LENGTH),
            each(1, WIDTH, HALF),
            each(1, WIDTH, HALF),
            each(1, HALF, WIDTH),
            whole(8, HALF),
        ],
        compiler_params=params,
        cost_estimate=pl.CostEstimate(
            flops=2 * 8 * 512 * 256 * 768, bytes_accessed=9 * 2**20, transcendentals=0
        ),
    )(
        homolog,
        other,
        mask_t,
        mask,
        other_mask,
        row_gain.reshape(1, WIDTH),
        row_in[:, WIDTH : 2 * WIDTH],
        row_in_t,
    )

    after_rows = pl.pallas_call(
        row_kernel,
        grid=(8 // BATCH,),
        out_shape=jax.ShapeDtypeStruct((PEERS, 40, WIDTH), BF16),
        in_specs=[
            whole(PEERS, 64, 256),
            each(BATCH, LENGTH, WIDTH + 128),
            each(BATCH, WIDTH, LENGTH),
            each(BATCH, WIDTH, HALF),
            each(BATCH, WIDTH, HALF),
            each(BATCH, HALF, WIDTH),
            whole(WIDTH, WIDTH),
            whole(8, HALF),
        ],
        out_specs=whole(PEERS, 40, WIDTH),
        scratch_shapes=[
            pltpu.VMEM((HEADS, LENGTH, HALF), F32),
            pltpu.VMEM((2, 8 * HALF, 128), F32),
        ],
        compiler_params=params,
        cost_estimate=pl.CostEstimate(
            flops=2 * 8 * 8 * 512 * 256 * 512, bytes_accessed=9 * 2**20, transcendentals=8 * 2**20
        ),
    )(tiles, keys, vt, qt, gt, xq, row_out, mask_half)

    columns = lax.all_to_all(after_rows, PLANE, 0, 0, tiled=True)

    finished = pl.pallas_call(
        column_kernel,
        grid=(4,),
        out_shape=jax.ShapeDtypeStruct((4 * LENGTH, WIDTH), BF16),
        in_specs=[
            whole(PEERS, 40, WIDTH),
            whole(1, WIDTH),
            whole(WIDTH, WIDTH),
            whole(4 * WIDTH, WIDTH),
            whole(WIDTH, WIDTH),
            whole(1, WIDTH),
            whole(WIDTH, 4 * WIDTH),
            whole(4 * WIDTH, WIDTH),
        ],
        out_specs=whole(4 * LENGTH, WIDTH),
        scratch_shapes=[
            pltpu.VMEM((PEERS, 5, 8, WIDTH), F32),
            pltpu.VMEM((2, 4 * LENGTH, 128), F32),
        ],
        compiler_params=params,
        cost_estimate=pl.CostEstimate(
            flops=2 * 8 * 8 * 512 * 256 * 512, bytes_accessed=4 * 2**20, transcendentals=8 * 2**20
        ),
    )(
        columns,
        col_gain.reshape(1, WIDTH),
        col_in[:, WIDTH : 2 * WIDTH],
        col_in_t,
        col_out,
        ff_gain.reshape(1, WIDTH),
        ff_expand,
        ff_shrink,
    )

    back = lax.all_to_all(finished.reshape(128, 16, WIDTH), AXES, 0, 0, tiled=True)
    back = back.reshape(32, 2, 2, 4, 4, WIDTH)
    return jnp.transpose(back, (3, 0, 2, 1, 4, 5)).reshape(4, LENGTH, WIDTH)


def solution(mesh):
    inner = Mesh(mesh.devices.reshape(2, 4, 4, 2, 2), AXES)
    dap = ("z", "x", "yh", "core")
    return jax.shard_map(
        body,
        mesh=inner,
        in_specs=(P(AXES, None, None), P(dap, "grp", None), P(AXES, None)) + (P(),) * 13,
        out_specs=P(AXES, None, None),
        check_vma=False,
    )
```

```python
import functools
import math

import jax
import jax.numpy as jnp
import ml_dtypes
import numpy as np
from jax import lax
from jax.experimental import pallas as pl
from jax.experimental.pallas import tpu as pltpu
from jax.sharding import Mesh, PartitionSpec as P

EPSILON = 1e-05
HEADS = 8
HEAD = 32
WIDTH = 256
LENGTH = 512
HALF = 256
PEERS = 64
LOG2E = math.log2(math.e)
SCALE = HEAD**-0.5 * LOG2E
F32 = jnp.float32
BF16 = jnp.bfloat16
AXES = ("grp", "z", "x", "yh", "core")
PLANE = ("grp", "z", "x", "yh")
VMEM_LIMIT = 40 * 1024 * 1024
SLOTS = 3
VMEM_WHOLE = 60 * 2**20
VMEM_TILE = 58 * 2**20
ROW_BOUND = 40.0
COLUMN_BOUND = 60.0

MASK_TERM = 1e9 * HEAD**0.5


def mask_parts():
    parts = []
    rest = MASK_TERM
    for _ in range(3):
        part = float(np.asarray(rest, ml_dtypes.bfloat16))
        parts.append(part)
        rest -= part
    return parts


def nt(a, b):
    return lax.dot_general(a, b, (((1,), (1,)), ((), ())), preferred_element_type=F32)


def tn(a, b):
    return lax.dot_general(a, b, (((0,), (0,)), ((), ())), preferred_element_type=F32)


def nn(a, b):
    return jnp.dot(a, b, preferred_element_type=F32)


def norm(x, gain):
    average = jnp.mean(x, axis=-1, keepdims=True)
    center = x - average
    spread = jnp.mean(center * center, axis=-1, keepdims=True)
    return (center * lax.rsqrt(spread + EPSILON) * gain).astype(BF16)


def position():
    q = (lax.axis_index("z") * 4 + lax.axis_index("x")) * 2 + lax.axis_index("yh")
    return lax.axis_index("grp"), q, lax.axis_index("core")


def bias_kernel(pair_ref, gain_ref, weight_ref, chain_ref, inter_ref, out_ref):
    grp, q, core = position()
    normed = norm(pair_ref[...].astype(F32), gain_ref[...])
    bias = nt(weight_ref[...], normed)
    chain = chain_ref[...]
    cols = jnp.where(grp == 0, chain[:, :256], chain[:, 256:])
    place = lax.broadcasted_iota(jnp.int32, (8, LENGTH), 1)
    wanted = 16 * q + 8 * core + lax.broadcasted_iota(jnp.int32, (8, LENGTH), 0)
    rows = jnp.sum(jnp.where(place == wanted, chain, 0), axis=1, keepdims=True)
    cross = (rows != cols).astype(F32)
    row = lax.broadcasted_iota(jnp.int32, (8, 8), 0)
    col = lax.broadcasted_iota(jnp.int32, (8, 8), 1)
    inter = jnp.sum(jnp.where(row == col, inter_ref[...], 0.0), axis=1, keepdims=True)
    parts = [
        bias[:, ii * 256 : (ii + 1) * 256] + inter * cross[ii : ii + 1] for ii in range(8)
    ]
    stacked = jnp.stack(parts, axis=0)
    tile = jnp.swapaxes(stacked, 0, 1).reshape(64, 256).astype(BF16)

    def put(p, carry):
        out_ref[p] = tile
        return carry

    lax.fori_loop(0, PEERS, put, 0)


def spread(qt, h, mask_rows):
    at = h % 4
    queries = qt.shape[1]
    pieces = []
    if at:
        pieces.append(jnp.zeros((HEAD * at, queries), BF16))
    pieces.append(qt[h * HEAD : (h + 1) * HEAD])
    if at < 3:
        pieces.append(jnp.zeros((HEAD * (3 - at), queries), BF16))
    pieces.append(mask_rows)
    return jnp.concatenate(pieces, axis=0)


def augment(keys, mask_tile):
    return [jnp.concatenate([keys[:, g * 128 : (g + 1) * 128], mask_tile], axis=1) for g in range(2)]


def score_bound(keys, qt):
    feat = lax.broadcasted_iota(jnp.int32, (WIDTH, 128), 0) // HEAD
    lane = lax.broadcasted_iota(jnp.int32, (WIDTH, 128), 1)
    ones = (feat == lane).astype(F32).astype(BF16)
    feat_t = lax.broadcasted_iota(jnp.int32, (16, WIDTH), 1) // HEAD
    row_t = lax.broadcasted_iota(jnp.int32, (16, WIDTH), 0)
    ones_t = (feat_t == row_t).astype(F32).astype(BF16)
    key_norm = jnp.max(nn(keys * keys, ones))
    query_norm = jnp.max(nn(ones_t, qt * qt))
    return jnp.sqrt(key_norm * 1.02) * jnp.sqrt(query_norm * 1.02) * SCALE


def any_present(tile):
    lane = lax.broadcasted_iota(jnp.int32, tile.shape, 1)
    return jnp.max(jnp.where(lane == 0, tile, -1e30)) > -1.0


def score_powers(keys, mask_tile, qt):
    mask_rows = jnp.ones((128, qt.shape[1]), BF16)
    augmented = augment(keys, mask_tile)
    out = []
    scores = nn(augmented[0], spread(qt, 0, mask_rows))
    for h in range(HEADS):
        later = None
        if h + 1 < HEADS:
            later = nn(augmented[(h + 1) // 4], spread(qt, h + 1, mask_rows))
        out.append(jnp.exp2(scores * SCALE).astype(BF16))
        scores = later
    return out


def blend(vt, h, powers):
    ones_v = jnp.ones((16, LENGTH), BF16)
    blended = nn(jnp.concatenate([vt[h * HEAD : (h + 1) * HEAD], ones_v], axis=0), powers)
    return blended[:HEAD] / blended[HEAD : HEAD + 1]


def attend(parts, bias, exact):
    mask_rows = jnp.ones((128, HALF), BF16)
    augmented = [augment(keys, tile) for keys, tile, _, _ in parts]
    units = [(part, h) for part in range(len(parts)) for h in range(HEADS)]

    def score(part, h):
        return nn(augmented[part][h // 4], spread(parts[part][3], h, mask_rows))

    out = []
    scores = score(*units[0])
    powers = None
    for at, (part, h) in enumerate(units):
        later = score(*units[at + 1]) if at + 1 < len(units) else None
        scaled = scores * SCALE
        if bias is not None:
            scaled = scaled + bias[h]
        if exact:
            scaled = scaled - jnp.max(scaled, axis=0, keepdims=True)
        now = jnp.exp2(scaled).astype(BF16)
        if at:
            before = units[at - 1]
            out.append(blend(parts[before[0]][2], before[1], powers))
        powers = now
        scores = later
    out.append(blend(parts[units[-1][0]][2], units[-1][1], powers))
    return [
        jnp.concatenate(out[part * HEADS : (part + 1) * HEADS], axis=0)
        for part in range(len(parts))
    ]


def project_kernel(
    own_ref, other_ref, mask_ref, own_mask_ref, other_mask_ref, gain_ref, wk_ref, wt_ref,
    k_ref, vt_ref, qt_ref, gt_ref, xq_ref, mask_out_ref, powers_ref, safe_ref,
):
    step = pl.program_id(0)
    _, _, core = position()
    x = jnp.where(step < 4, own_ref[0].astype(F32), other_ref[0].astype(F32))
    normed = norm(x, gain_ref[...])
    keys = nn(normed, wk_ref[...]).astype(BF16)
    k_ref[0, :, :WIDTH] = keys
    lane = lax.broadcasted_iota(jnp.int32, (8, 128), 1)
    row = lax.broadcasted_iota(jnp.int32, (8, 128), 0)
    consts = mask_parts()
    pick = jnp.zeros((8, 128), F32)
    for at, value in enumerate(consts):
        pick = jnp.where((lane == at) & (row == step), value, pick)
    tile = nn(mask_ref[...] - 1, pick.astype(BF16))
    mask_tile = tile.astype(BF16)
    k_ref[0, :, WIDTH:] = mask_tile
    vt_ref[0] = nt(wt_ref[2 * WIDTH : 3 * WIDTH], normed).astype(BF16)

    def half(a):
        rows = a.reshape(32, 2, 8, WIDTH)
        return jnp.where(core == 0, rows[:, 0], rows[:, 1]).reshape(HALF, WIDTH)

    xq = half(x)
    xq_ref[0] = xq.astype(BF16)
    normed_q = half(normed.astype(F32)).astype(BF16)
    qt = nt(wt_ref[:WIDTH], normed_q).astype(BF16)
    qt_ref[0] = qt
    powers = score_powers(keys, mask_tile, qt)
    for h in range(HEADS):
        powers_ref[0, h] = powers[h]
    bound = score_bound(keys, qt)
    present = any_present(tile)
    safe = (bound <= ROW_BOUND) & present
    safe_ref[0] = jnp.where(safe, 1.0, 0.0) + jnp.zeros((8, 128), F32)
    gt_ref[0] = nt(wt_ref[3 * WIDTH :], normed_q).astype(BF16)

    @pl.when(step == 0)
    def _():
        own = own_mask_ref[...].astype(F32)
        other = other_mask_ref[...].astype(F32)
        first = jnp.where(core == 0, own, other)
        second = jnp.where(core == 0, other, own)
        mask = jnp.concatenate([first, second], axis=0).astype(BF16)
        i = lax.broadcasted_iota(jnp.int32, (LENGTH, HALF), 0)
        l = lax.broadcasted_iota(jnp.int32, (LENGTH, HALF), 1)
        pick = (i == (l // 8) * 16 + core * 8 + l % 8).astype(F32).astype(BF16)
        mask_out_ref[...] = nn(mask, pick).astype(BF16)


def bias_blocks(tile_ref):
    row = lax.broadcasted_iota(jnp.int32, (HALF, HALF), 0)
    col = lax.broadcasted_iota(jnp.int32, (HALF, HALF), 1)
    eye = (row == col).astype(F32).astype(BF16)
    for g in range(2):
        for pair in range(4):
            block = tile_ref[g * 32 : (g + 1) * 32, pair * 16 : (pair + 1) * 16, :]
            block = block.astype(F32).reshape(32, 2, 8, 256)
            for k in range(2):
                rows = block[:, k].reshape(HALF, 256).astype(BF16)
                yield pair * 2 + k, g, nt(eye, rows) * LOG2E


def row_kernel(
    safe_ref, wo_ref, mask_ref, tile_ref, powers_ref, vt_ref, gt_ref, xq_ref, k_ref, qt_ref,
    out_ref, powers_here, vt_here, gt_here, xq_here, bias_ref, factor_ref, o_ref, y_ref, result_ref,
    k_here, qt_here, slot_sem, out_sem,
):
    _, _, core = position()

    def fetch(step):
        slot = lax.rem(step, SLOTS)
        pairs = [(powers_ref, powers_here), (vt_ref, vt_here), (gt_ref, gt_here), (xq_ref, xq_here)]
        return [
            pltpu.make_async_copy(source.at[step], target.at[slot], slot_sem.at[slot, n])
            for n, (source, target) in enumerate(pairs)
        ]

    for step in range(SLOTS):
        for copy in fetch(step):
            copy.start()

    largest = jnp.zeros((8, HALF), F32)
    for h, g, block in bias_blocks(tile_ref):
        factor_ref[h, g * 256 : (g + 1) * 256, :] = jnp.exp2(block).astype(BF16)
        size = jnp.abs(block).reshape(32, 8, HALF)
        largest = jnp.maximum(largest, jnp.max(size, axis=0))
    bias_safe = jnp.max(largest) <= ROW_BOUND

    def sequence(step, carry):
        slot = lax.rem(step, SLOTS)
        for copy in fetch(step):
            copy.wait()
        safe = bias_safe & (jnp.max(safe_ref[step]) > 0.5)

        @pl.when(safe)
        def _():
            now = powers_here[slot, 0] * factor_ref[0]
            for h in range(HEADS):
                later = None
                if h + 1 < HEADS:
                    later = powers_here[slot, h + 1] * factor_ref[h + 1]
                o_ref[h * HEAD : (h + 1) * HEAD, :] = blend(vt_here[slot], h, now)
                now = later

        @pl.when(jnp.logical_not(safe))
        def _():
            pltpu.sync_copy(k_ref.at[step], k_here)
            pltpu.sync_copy(qt_ref.at[step], qt_here)
            for h, g, block in bias_blocks(tile_ref):
                bias_ref[h, g * 256 : (g + 1) * 256, :] = block
            part = (k_here[:, :WIDTH], k_here[:, WIDTH:], vt_here[slot], qt_here[...])
            o_ref[...] = attend([part], bias_ref, True)[0]

        gated = (o_ref[...] * jax.nn.sigmoid(gt_here[slot].astype(F32))).astype(BF16)
        y = xq_here[slot].astype(F32) + tn(gated, wo_ref[...])
        s = lax.rem(step + 4 * core, 8)
        for j in range(2):
            y_ref[j, pl.ds(s, HALF, stride=8), :] = y[:, j * 128 : (j + 1) * 128]

        @pl.when(step + SLOTS < 8)
        def _():
            for copy in fetch(step + SLOTS):
                copy.start()

        return carry

    lax.fori_loop(0, 8, sequence, 0)
    for j in range(2):
        result_ref[:, j * 32 : (j + 1) * 32, :] = y_ref[j].astype(BF16).reshape(PEERS, 32, 128)
        result_ref[j * 32 : (j + 1) * 32, 64:, :] = jnp.broadcast_to(
            mask_ref[:, j * 128 : (j + 1) * 128][None], (32, 8, 128)
        )
    out = pltpu.make_async_copy(result_ref, out_ref, out_sem)
    out.start()
    out.wait()


def column_kernel(
    x_ref, gain_ref, wk_ref, wt_ref, wo_ref, gain2_ref, w1_ref, w2_ref, out_ref,
    x32_ref, o_ref, y_ref,
):
    _, q, _ = position()
    x32_ref[...] = x_ref[...].astype(F32).reshape(PEERS, 9, 8, 128)

    def residue(r, carry):
        x = jnp.concatenate([x32_ref[:, 4 * j + r].reshape(LENGTH, 128) for j in range(2)], axis=1)
        normed = norm(x, gain_ref[...])
        keys = nn(normed, wk_ref[...]).astype(BF16)
        lane = lax.broadcasted_iota(jnp.int32, (128, 128), 1)
        row = lax.broadcasted_iota(jnp.int32, (128, 128), 0)
        pick = jnp.zeros((128, 128), F32)
        for at, value in enumerate(mask_parts()):
            pick = jnp.where((lane == at) & (row == 4 * q + r), value, pick)
        absent = (x32_ref[:, 8].reshape(LENGTH, 128) - 1.0).astype(BF16)
        tile = nn(absent, pick.astype(BF16))
        mask_tile = tile.astype(BF16)
        vt = nt(wt_ref[2 * WIDTH : 3 * WIDTH], normed).astype(BF16)
        qt = nt(wt_ref[:WIDTH], normed).astype(BF16)
        gt = nt(wt_ref[3 * WIDTH :], normed).astype(BF16)
        parts = [(keys, mask_tile, vt, qt[:, n * HALF : (n + 1) * HALF]) for n in range(2)]
        safe = (score_bound(keys, qt) <= COLUMN_BOUND) & any_present(tile)

        @pl.when(safe)
        def _():
            for n, o in enumerate(attend(parts, None, False)):
                o_ref[n] = o

        @pl.when(jnp.logical_not(safe))
        def _():
            for n, o in enumerate(attend(parts, None, True)):
                o_ref[n] = o

        for n in range(2):
            cols = slice(n * HALF, (n + 1) * HALF)
            gated = (o_ref[n] * jax.nn.sigmoid(gt[:, cols].astype(F32))).astype(BF16)
            one = x[cols] + tn(gated, wo_ref[...])
            two = one.astype(BF16).astype(F32)
            hidden = jnp.maximum(nn(norm(two, gain2_ref[...]), w1_ref[...]), 0.0).astype(BF16)
            y = two + nn(hidden, w2_ref[...])
            for j in range(2):
                y_ref[j, pl.ds(n * 4 * HALF + r, HALF, stride=4), :] = y[:, j * 128 : (j + 1) * 128]
        return carry

    lax.fori_loop(0, 4, residue, 0)
    for j in range(2):
        out_ref[:, j * 128 : (j + 1) * 128] = y_ref[j].astype(BF16)


def whole(*shape):
    return pl.BlockSpec(shape, lambda i: (0,) * len(shape))


def each(count, *shape):
    return pl.BlockSpec((count,) + shape, lambda i: (i,) + (0,) * len(shape))


def body(
    homolog,
    pair_state,
    mask,
    chain,
    row_gain,
    pair_gain,
    pair_weight,
    interchain,
    row_in,
    row_out,
    col_gain,
    col_in,
    col_out,
    ff_gain,
    ff_expand,
    ff_shrink,
):
    params = pltpu.CompilerParams(vmem_limit_bytes=VMEM_LIMIT)
    here = pl.BlockSpec(memory_space=pltpu.VMEM)
    away = pl.BlockSpec(memory_space=pltpu.HBM)
    swap = [(0, 1), (1, 0)]
    other_mask = lax.ppermute(mask, "core", swap)
    other = lax.ppermute(homolog, "core", swap)

    payload = pl.pallas_call(
        bias_kernel,
        grid=(1,),
        out_shape=jax.ShapeDtypeStruct((PEERS, 64, 256), BF16),
        in_specs=[whole(2048, 128), whole(1, 128), whole(8, 128), whole(1, LENGTH), whole(1, 8)],
        out_specs=whole(PEERS, 64, 256),
        compiler_params=pltpu.CompilerParams(vmem_limit_bytes=VMEM_WHOLE),
    )(
        pair_state.reshape(2048, 128),
        pair_gain.reshape(1, 128),
        pair_weight,
        chain.reshape(1, LENGTH),
        interchain.reshape(1, 8),
    )
    tiles = lax.all_to_all(payload, PLANE, 0, 0, tiled=True)

    row_in_t = row_in.T
    col_in_t = col_in.T
    mask_t = jnp.concatenate([mask, other_mask], axis=0).astype(BF16).T
    keys, vt, qt, gt, xq, mask_half, powers, safe = pl.pallas_call(
        project_kernel,
        grid=(8,),
        out_shape=[
            jax.ShapeDtypeStruct((8, LENGTH, WIDTH + 128), BF16),
            jax.ShapeDtypeStruct((8, WIDTH, LENGTH), BF16),
            jax.ShapeDtypeStruct((8, WIDTH, HALF), BF16),
            jax.ShapeDtypeStruct((8, WIDTH, HALF), BF16),
            jax.ShapeDtypeStruct((8, HALF, WIDTH), BF16),
            jax.ShapeDtypeStruct((8, HALF), BF16),
            jax.ShapeDtypeStruct((8, HEADS, LENGTH, HALF), BF16),
            jax.ShapeDtypeStruct((8, 8, 128), F32),
        ],
        in_specs=[
            pl.BlockSpec((1, LENGTH, WIDTH), lambda i: (jnp.minimum(i, 3), 0, 0)),
            pl.BlockSpec((1, LENGTH, WIDTH), lambda i: (jnp.maximum(i - 4, 0), 0, 0)),
            whole(LENGTH, 8),
            whole(4, LENGTH),
            whole(4, LENGTH),
            whole(1, WIDTH),
            whole(WIDTH, WIDTH),
            whole(4 * WIDTH, WIDTH),
        ],
        out_specs=[
            each(1, LENGTH, WIDTH + 128),
            each(1, WIDTH, LENGTH),
            each(1, WIDTH, HALF),
            each(1, WIDTH, HALF),
            each(1, HALF, WIDTH),
            whole(8, HALF),
            each(1, HEADS, LENGTH, HALF),
            each(1, 8, 128),
        ],
        compiler_params=pltpu.CompilerParams(vmem_limit_bytes=VMEM_WHOLE),
        cost_estimate=pl.CostEstimate(
            flops=8 * 8 * 512 * 256 * 768, bytes_accessed=25 * 2**20, transcendentals=8 * 2**20
        ),
    )(
        homolog,
        other,
        mask_t,
        mask,
        other_mask,
        row_gain.reshape(1, WIDTH),
        row_in[:, WIDTH : 2 * WIDTH],
        row_in_t,
    )

    after_rows = pl.pallas_call(
        row_kernel,
        out_shape=jax.ShapeDtypeStruct((PEERS, 72, 128), BF16),
        grid=(1,),
        in_specs=[whole(8, 8, 128), whole(WIDTH, WIDTH), whole(8, HALF), here] + [away] * 6,
        out_specs=away,
        scratch_shapes=[
            pltpu.VMEM((SLOTS, HEADS, LENGTH, HALF), BF16),
            pltpu.VMEM((SLOTS, WIDTH, LENGTH), BF16),
            pltpu.VMEM((SLOTS, WIDTH, HALF), BF16),
            pltpu.VMEM((SLOTS, HALF, WIDTH), BF16),
            pltpu.VMEM((HEADS, LENGTH, HALF), F32),
            pltpu.VMEM((HEADS, LENGTH, HALF), BF16),
            pltpu.VMEM((WIDTH, HALF), F32),
            pltpu.VMEM((2, 8 * HALF, 128), F32),
            pltpu.VMEM((PEERS, 72, 128), BF16),
            pltpu.VMEM((LENGTH, WIDTH + 128), BF16),
            pltpu.VMEM((WIDTH, HALF), BF16),
            pltpu.SemaphoreType.DMA((SLOTS, 4)),
            pltpu.SemaphoreType.DMA,
        ],
        compiler_params=pltpu.CompilerParams(vmem_limit_bytes=VMEM_TILE),
        cost_estimate=pl.CostEstimate(
            flops=8 * 8 * 512 * 256 * 512, bytes_accessed=20 * 2**20, transcendentals=0
        ),
    )(safe, row_out, mask_half, tiles, powers, vt, gt, xq, keys, qt)

    columns = lax.all_to_all(after_rows, PLANE, 0, 0, tiled=True)

    finished = pl.pallas_call(
        column_kernel,
        out_shape=jax.ShapeDtypeStruct((4 * LENGTH, WIDTH), BF16),
        grid=(1,),
        in_specs=[here] * 8,
        out_specs=whole(4 * LENGTH, WIDTH),
        scratch_shapes=[
            pltpu.VMEM((PEERS, 9, 8, 128), F32),
            pltpu.VMEM((2, WIDTH, HALF), F32),
            pltpu.VMEM((2, 4 * LENGTH, 128), F32),
        ],
        compiler_params=params,
        cost_estimate=pl.CostEstimate(
            flops=2 * 8 * 8 * 512 * 256 * 512, bytes_accessed=4 * 2**20, transcendentals=8 * 2**20
        ),
    )(
        columns,
        col_gain.reshape(1, WIDTH),
        col_in[:, WIDTH : 2 * WIDTH],
        col_in_t,
        col_out,
        ff_gain.reshape(1, WIDTH),
        ff_expand,
        ff_shrink,
    )

    back = lax.all_to_all(finished.reshape(128, 16, WIDTH), AXES, 0, 0, tiled=True)
    back = back.reshape(32, 2, 2, 4, 4, WIDTH)
    return jnp.transpose(back, (3, 0, 2, 1, 4, 5)).reshape(4, LENGTH, WIDTH)


def solution(mesh):
    inner = Mesh(mesh.devices.reshape(2, 4, 4, 2, 2), AXES)
    dap = ("z", "x", "yh", "core")
    return jax.shard_map(
        body,
        mesh=inner,
        in_specs=(P(AXES, None, None), P(dap, "grp", None), P(AXES, None)) + (P(),) * 13,
        out_specs=P(AXES, None, None),
        check_vma=False,
    )
```

```python
import functools
import math

import jax
import jax.numpy as jnp
import ml_dtypes
import numpy as np
from jax import lax
from jax.experimental import pallas as pl
from jax.experimental.pallas import tpu as pltpu
from jax.sharding import Mesh, PartitionSpec as P

EPSILON = 1e-05
HEADS = 8
HEAD = 32
WIDTH = 256
LENGTH = 512
HALF = 256
PEERS = 64
LOG2E = math.log2(math.e)
SCALE = HEAD**-0.5 * LOG2E
F32 = jnp.float32
BF16 = jnp.bfloat16
AXES = ("grp", "z", "x", "yh", "core")
PLANE = ("grp", "z", "x", "yh")
VMEM_LIMIT = 40 * 1024 * 1024
SLOTS = 3
VMEM_WHOLE = 60 * 2**20
VMEM_TILE = 58 * 2**20
ROW_BOUND = 40.0
COLUMN_BOUND = 60.0

MASK_TERM = 1e9 * HEAD**0.5


def mask_parts():
    parts = []
    rest = MASK_TERM
    for _ in range(3):
        part = float(np.asarray(rest, ml_dtypes.bfloat16))
        parts.append(part)
        rest -= part
    return parts


def nt(a, b):
    return lax.dot_general(a, b, (((1,), (1,)), ((), ())), preferred_element_type=F32)


def tn(a, b):
    return lax.dot_general(a, b, (((0,), (0,)), ((), ())), preferred_element_type=F32)


def nn(a, b):
    return jnp.dot(a, b, preferred_element_type=F32)


def norm(x, gain):
    average = jnp.mean(x, axis=-1, keepdims=True)
    center = x - average
    spread = jnp.mean(center * center, axis=-1, keepdims=True)
    return (center * lax.rsqrt(spread + EPSILON) * gain).astype(BF16)


def position():
    q = (lax.axis_index("z") * 4 + lax.axis_index("x")) * 2 + lax.axis_index("yh")
    return lax.axis_index("grp"), q, lax.axis_index("core")


def bias_kernel(pair_ref, gain_ref, weight_ref, chain_ref, inter_ref, out_ref):
    grp, q, core = position()
    normed = norm(pair_ref[...].astype(F32), gain_ref[...])
    bias = nt(weight_ref[...], normed)
    chain = chain_ref[...]
    cols = jnp.where(grp == 0, chain[:, :256], chain[:, 256:])
    place = lax.broadcasted_iota(jnp.int32, (8, LENGTH), 1)
    wanted = 16 * q + 8 * core + lax.broadcasted_iota(jnp.int32, (8, LENGTH), 0)
    rows = jnp.sum(jnp.where(place == wanted, chain, 0), axis=1, keepdims=True)
    cross = (rows != cols).astype(F32)
    row = lax.broadcasted_iota(jnp.int32, (8, 8), 0)
    col = lax.broadcasted_iota(jnp.int32, (8, 8), 1)
    inter = jnp.sum(jnp.where(row == col, inter_ref[...], 0.0), axis=1, keepdims=True)
    parts = [
        bias[:, ii * 256 : (ii + 1) * 256] + inter * cross[ii : ii + 1] for ii in range(8)
    ]
    stacked = jnp.stack(parts, axis=0)
    tile = jnp.swapaxes(stacked, 0, 1).reshape(64, 256).astype(BF16)

    def put(p, carry):
        out_ref[p] = tile
        return carry

    lax.fori_loop(0, PEERS, put, 0)


def spread(qt, h, mask_rows):
    at = h % 4
    queries = qt.shape[1]
    pieces = []
    if at:
        pieces.append(jnp.zeros((HEAD * at, queries), BF16))
    pieces.append(qt[h * HEAD : (h + 1) * HEAD])
    if at < 3:
        pieces.append(jnp.zeros((HEAD * (3 - at), queries), BF16))
    pieces.append(mask_rows)
    return jnp.concatenate(pieces, axis=0)


def augment(keys, mask_tile):
    return [jnp.concatenate([keys[:, g * 128 : (g + 1) * 128], mask_tile], axis=1) for g in range(2)]


def score_bound(keys, qt):
    feat = lax.broadcasted_iota(jnp.int32, (WIDTH, 128), 0) // HEAD
    lane = lax.broadcasted_iota(jnp.int32, (WIDTH, 128), 1)
    ones = (feat == lane).astype(F32).astype(BF16)
    feat_t = lax.broadcasted_iota(jnp.int32, (16, WIDTH), 1) // HEAD
    row_t = lax.broadcasted_iota(jnp.int32, (16, WIDTH), 0)
    ones_t = (feat_t == row_t).astype(F32).astype(BF16)
    key_norm = jnp.max(nn(keys * keys, ones))
    query_norm = jnp.max(nn(ones_t, qt * qt))
    return jnp.sqrt(key_norm * 1.02) * jnp.sqrt(query_norm * 1.02) * SCALE


def any_present(tile):
    lane = lax.broadcasted_iota(jnp.int32, tile.shape, 1)
    return jnp.max(jnp.where(lane == 0, tile, -1e30)) > -1.0


def score_powers(keys, mask_tile, qt):
    mask_rows = jnp.ones((128, qt.shape[1]), BF16)
    augmented = augment(keys, mask_tile)
    out = []
    scores = nn(augmented[0], spread(qt, 0, mask_rows))
    for h in range(HEADS):
        later = None
        if h + 1 < HEADS:
            later = nn(augmented[(h + 1) // 4], spread(qt, h + 1, mask_rows))
        out.append(jnp.exp2(scores * SCALE).astype(BF16))
        scores = later
    return out


def blend(vt, h, powers):
    ones_v = jnp.ones((16, LENGTH), BF16)
    blended = nn(jnp.concatenate([vt[h * HEAD : (h + 1) * HEAD], ones_v], axis=0), powers)
    return blended[:HEAD] / blended[HEAD : HEAD + 1]


def attend(parts, bias, exact, between=()):
    mask_rows = jnp.ones((128, HALF), BF16)
    augmented = [augment(keys, tile) for keys, tile, _, _ in parts]
    units = [(part, h) for part in range(len(parts)) for h in range(HEADS)]

    def score(part, h):
        return nn(augmented[part][h // 4], spread(parts[part][3], h, mask_rows))

    out = []
    scores = score(*units[0])
    powers = None
    for at, (part, h) in enumerate(units):
        later = score(*units[at + 1]) if at + 1 < len(units) else None
        scaled = scores * SCALE
        if bias is not None:
            scaled = scaled + bias[h]
        if exact:
            scaled = scaled - jnp.max(scaled, axis=0, keepdims=True)
        now = jnp.exp2(scaled).astype(BF16)
        if at:
            before = units[at - 1]
            out.append(blend(parts[before[0]][2], before[1], powers))
        powers = now
        scores = later
        for call in between[at * len(between) // len(units) : (at + 1) * len(between) // len(units)]:
            call()
    out.append(blend(parts[units[-1][0]][2], units[-1][1], powers))
    return [
        jnp.concatenate(out[part * HEADS : (part + 1) * HEADS], axis=0)
        for part in range(len(parts))
    ]


def project_kernel(
    own_ref, other_ref, mask_ref, own_mask_ref, other_mask_ref, gain_ref, wk_ref, wt_ref,
    k_ref, vt_ref, qt_ref, gt_ref, xq_ref, mask_out_ref, powers_ref, safe_ref,
):
    step = pl.program_id(0)
    _, _, core = position()
    x = jnp.where(step < 4, own_ref[0].astype(F32), other_ref[0].astype(F32))
    normed = norm(x, gain_ref[...])
    keys = nn(normed, wk_ref[...]).astype(BF16)
    k_ref[0, :, :WIDTH] = keys
    lane = lax.broadcasted_iota(jnp.int32, (8, 128), 1)
    row = lax.broadcasted_iota(jnp.int32, (8, 128), 0)
    consts = mask_parts()
    pick = jnp.zeros((8, 128), F32)
    for at, value in enumerate(consts):
        pick = jnp.where((lane == at) & (row == step), value, pick)
    tile = nn(mask_ref[...] - 1, pick.astype(BF16))
    mask_tile = tile.astype(BF16)
    k_ref[0, :, WIDTH:] = mask_tile
    vt_ref[0] = nt(wt_ref[2 * WIDTH : 3 * WIDTH], normed).astype(BF16)

    def half(a):
        rows = a.reshape(32, 2, 8, WIDTH)
        return jnp.where(core == 0, rows[:, 0], rows[:, 1]).reshape(HALF, WIDTH)

    xq = half(x)
    xq_ref[0] = xq.astype(BF16)
    normed_q = half(normed.astype(F32)).astype(BF16)
    qt = nt(wt_ref[:WIDTH], normed_q).astype(BF16)
    qt_ref[0] = qt
    powers = score_powers(keys, mask_tile, qt)
    for h in range(HEADS):
        powers_ref[0, h] = powers[h]
    bound = score_bound(keys, qt)
    present = any_present(tile)
    safe = (bound <= ROW_BOUND) & present
    safe_ref[0] = jnp.where(safe, 1.0, 0.0) + jnp.zeros((8, 128), F32)
    gt_ref[0] = nt(wt_ref[3 * WIDTH :], normed_q).astype(BF16)

    @pl.when(step == 0)
    def _():
        own = own_mask_ref[...].astype(F32)
        other = other_mask_ref[...].astype(F32)
        first = jnp.where(core == 0, own, other)
        second = jnp.where(core == 0, other, own)
        mask = jnp.concatenate([first, second], axis=0).astype(BF16)
        i = lax.broadcasted_iota(jnp.int32, (LENGTH, HALF), 0)
        l = lax.broadcasted_iota(jnp.int32, (LENGTH, HALF), 1)
        pick = (i == (l // 8) * 16 + core * 8 + l % 8).astype(F32).astype(BF16)
        mask_out_ref[...] = nn(mask, pick).astype(BF16)


def bias_blocks(tile_ref):
    row = lax.broadcasted_iota(jnp.int32, (HALF, HALF), 0)
    col = lax.broadcasted_iota(jnp.int32, (HALF, HALF), 1)
    eye = (row == col).astype(F32).astype(BF16)
    for g in range(2):
        for pair in range(4):
            block = tile_ref[g * 32 : (g + 1) * 32, pair * 16 : (pair + 1) * 16, :]
            block = block.astype(F32).reshape(32, 2, 8, 256)
            for k in range(2):
                rows = block[:, k].reshape(HALF, 256).astype(BF16)
                yield pair * 2 + k, g, nt(eye, rows) * LOG2E


def row_kernel(
    safe_ref, wo_ref, mask_ref, tile_ref, powers_ref, vt_ref, gt_ref, xq_ref, k_ref, qt_ref,
    out_ref, powers_here, vt_here, gt_here, xq_here, bias_ref, factor_ref, o_ref, y_ref, result_ref,
    k_here, qt_here, slot_sem, out_sem,
):
    _, _, core = position()

    def fetch(step):
        slot = lax.rem(step, SLOTS)
        pairs = [(powers_ref, powers_here), (vt_ref, vt_here), (gt_ref, gt_here), (xq_ref, xq_here)]
        return [
            pltpu.make_async_copy(source.at[step], target.at[slot], slot_sem.at[slot, n])
            for n, (source, target) in enumerate(pairs)
        ]

    for step in range(SLOTS):
        for copy in fetch(step):
            copy.start()

    largest = jnp.zeros((8, HALF), F32)
    for h, g, block in bias_blocks(tile_ref):
        factor_ref[h, g * 256 : (g + 1) * 256, :] = jnp.exp2(block).astype(BF16)
        size = jnp.abs(block).reshape(32, 8, HALF)
        largest = jnp.maximum(largest, jnp.max(size, axis=0))
    bias_safe = jnp.max(largest) <= ROW_BOUND

    def sequence(step, carry):
        slot = lax.rem(step, SLOTS)
        for copy in fetch(step):
            copy.wait()
        safe = bias_safe & (jnp.max(safe_ref[step]) > 0.5)

        @pl.when(safe)
        def _():
            now = powers_here[slot, 0] * factor_ref[0]
            for h in range(HEADS):
                later = None
                if h + 1 < HEADS:
                    later = powers_here[slot, h + 1] * factor_ref[h + 1]
                o_ref[h * HEAD : (h + 1) * HEAD, :] = blend(vt_here[slot], h, now)
                now = later

        @pl.when(jnp.logical_not(safe))
        def _():
            pltpu.sync_copy(k_ref.at[step], k_here)
            pltpu.sync_copy(qt_ref.at[step], qt_here)
            for h, g, block in bias_blocks(tile_ref):
                bias_ref[h, g * 256 : (g + 1) * 256, :] = block
            part = (k_here[:, :WIDTH], k_here[:, WIDTH:], vt_here[slot], qt_here[...])
            o_ref[...] = attend([part], bias_ref, True)[0]

        gated = (o_ref[...] * jax.nn.sigmoid(gt_here[slot].astype(F32))).astype(BF16)
        y = xq_here[slot].astype(F32) + tn(gated, wo_ref[...])
        s = lax.rem(step + 4 * core, 8)
        for j in range(2):
            y_ref[j, pl.ds(s, HALF, stride=8), :] = y[:, j * 128 : (j + 1) * 128]

        @pl.when(step + SLOTS < 8)
        def _():
            for copy in fetch(step + SLOTS):
                copy.start()

        return carry

    lax.fori_loop(0, 8, sequence, 0)
    for j in range(2):
        result_ref[:, j * 32 : (j + 1) * 32, :] = y_ref[j].astype(BF16).reshape(PEERS, 32, 128)
        result_ref[j * 32 : (j + 1) * 32, 64:, :] = jnp.broadcast_to(
            mask_ref[:, j * 128 : (j + 1) * 128][None], (32, 8, 128)
        )
    out = pltpu.make_async_copy(result_ref, out_ref, out_sem)
    out.start()
    out.wait()


def column_kernel(
    x_ref, gain_ref, wk_ref, wt_ref, wo_ref, gain2_ref, w1_ref, w2_ref, out_ref,
    x32_ref, keys_ref, tile_ref, vt_ref, qt_ref, gt_ref, o_ref, total_ref, normed_ref, y_ref,
):
    _, q, _ = position()
    x32_ref[...] = x_ref[...].astype(F32).reshape(PEERS, 9, 8, 128)
    absent = (x32_ref[:, 8].reshape(LENGTH, 128) - 1.0).astype(BF16)
    lane = lax.broadcasted_iota(jnp.int32, (128, 128), 1)
    row = lax.broadcasted_iota(jnp.int32, (128, 128), 0)

    def residue_rows(r, first, count):
        halves = [
            x32_ref[first : first + count, 4 * j + r].reshape(count * 8, 128) for j in range(2)
        ]
        return jnp.concatenate(halves, axis=1)

    safe = jnp.bool_(True)
    for r in range(4):
        normed = norm(residue_rows(r, 0, PEERS), gain_ref[...])
        keys = nn(normed, wk_ref[...]).astype(BF16)
        keys_ref[r] = keys
        pick = jnp.zeros((128, 128), F32)
        for at, value in enumerate(mask_parts()):
            pick = jnp.where((lane == at) & (row == 4 * q + r), value, pick)
        tile = nn(absent, pick.astype(BF16))
        tile_ref[r] = tile.astype(BF16)
        vt_ref[r] = nt(wt_ref[2 * WIDTH : 3 * WIDTH], normed).astype(BF16)
        qt = nt(wt_ref[:WIDTH], normed).astype(BF16)
        qt_ref[r] = qt
        gt_ref[r] = nt(wt_ref[3 * WIDTH :], normed).astype(BF16)
        safe = safe & (score_bound(keys, qt) <= COLUMN_BOUND) & any_present(tile)

    def attention(r, exact, between=()):
        parts = [
            (keys_ref[r], tile_ref[r], vt_ref[r], qt_ref[r, :, n * HALF : (n + 1) * HALF])
            for n in range(2)
        ]
        for n, o in enumerate(attend(parts, None, exact, between)):
            cols = slice(n * HALF, (n + 1) * HALF)
            gate = jax.nn.sigmoid(gt_ref[r, :, cols].astype(F32))
            o_ref[r, :, cols] = (o * gate).astype(BF16)

    def project_out(r):
        one = residue_rows(r, 0, PEERS) + tn(o_ref[r], wo_ref[...])
        total_ref[...] = one.astype(BF16).astype(F32)

    def normalize():
        normed_ref[...] = norm(total_ref[...], gain2_ref[...])

    def transition(part):
        cols = slice(part * 256, (part + 1) * 256)
        hidden = jnp.maximum(nn(normed_ref[...], w1_ref[:, cols]), 0.0).astype(BF16)
        total_ref[...] += nn(hidden, w2_ref[cols])

    def keep(r):
        for j in range(2):
            y_ref[j, pl.ds(r, LENGTH, stride=4), :] = total_ref[:, j * 128 : (j + 1) * 128]

    def finishing(r):
        blocks = [functools.partial(transition, part) for part in range(4)]
        return [functools.partial(project_out, r), normalize] + blocks + [functools.partial(keep, r)]

    @pl.when(safe)
    def _():
        attention(0, False)

        def residue(r, carry):
            attention(r, False, finishing(r - 1))
            return carry

        lax.fori_loop(1, 4, residue, 0)

    @pl.when(jnp.logical_not(safe))
    def _():
        def residue(r, carry):
            attention(r, True)
            return carry

        lax.fori_loop(0, 4, residue, 0)

        def rest(r, carry):
            for call in finishing(r):
                call()
            return carry

        lax.fori_loop(0, 3, rest, 0)

    for call in finishing(3):
        call()
    for j in range(2):
        out_ref[:, j * 128 : (j + 1) * 128] = y_ref[j].astype(BF16)


def whole(*shape):
    return pl.BlockSpec(shape, lambda i: (0,) * len(shape))


def each(count, *shape):
    return pl.BlockSpec((count,) + shape, lambda i: (i,) + (0,) * len(shape))


def body(
    homolog,
    pair_state,
    mask,
    chain,
    row_gain,
    pair_gain,
    pair_weight,
    interchain,
    row_in,
    row_out,
    col_gain,
    col_in,
    col_out,
    ff_gain,
    ff_expand,
    ff_shrink,
):
    params = pltpu.CompilerParams(vmem_limit_bytes=VMEM_LIMIT)
    here = pl.BlockSpec(memory_space=pltpu.VMEM)
    away = pl.BlockSpec(memory_space=pltpu.HBM)
    swap = [(0, 1), (1, 0)]
    other_mask = lax.ppermute(mask, "core", swap)
    other = lax.ppermute(homolog, "core", swap)

    payload = pl.pallas_call(
        bias_kernel,
        grid=(1,),
        out_shape=jax.ShapeDtypeStruct((PEERS, 64, 256), BF16),
        in_specs=[whole(2048, 128), whole(1, 128), whole(8, 128), whole(1, LENGTH), whole(1, 8)],
        out_specs=whole(PEERS, 64, 256),
        compiler_params=pltpu.CompilerParams(vmem_limit_bytes=VMEM_WHOLE),
    )(
        pair_state.reshape(2048, 128),
        pair_gain.reshape(1, 128),
        pair_weight,
        chain.reshape(1, LENGTH),
        interchain.reshape(1, 8),
    )
    tiles = lax.all_to_all(payload, PLANE, 0, 0, tiled=True)

    row_in_t = row_in.T
    col_in_t = col_in.T
    mask_t = jnp.concatenate([mask, other_mask], axis=0).astype(BF16).T
    keys, vt, qt, gt, xq, mask_half, powers, safe = pl.pallas_call(
        project_kernel,
        grid=(8,),
        out_shape=[
            jax.ShapeDtypeStruct((8, LENGTH, WIDTH + 128), BF16),
            jax.ShapeDtypeStruct((8, WIDTH, LENGTH), BF16),
            jax.ShapeDtypeStruct((8, WIDTH, HALF), BF16),
            jax.ShapeDtypeStruct((8, WIDTH, HALF), BF16),
            jax.ShapeDtypeStruct((8, HALF, WIDTH), BF16),
            jax.ShapeDtypeStruct((8, HALF), BF16),
            jax.ShapeDtypeStruct((8, HEADS, LENGTH, HALF), BF16),
            jax.ShapeDtypeStruct((8, 8, 128), F32),
        ],
        in_specs=[
            pl.BlockSpec((1, LENGTH, WIDTH), lambda i: (jnp.minimum(i, 3), 0, 0)),
            pl.BlockSpec((1, LENGTH, WIDTH), lambda i: (jnp.maximum(i - 4, 0), 0, 0)),
            whole(LENGTH, 8),
            whole(4, LENGTH),
            whole(4, LENGTH),
            whole(1, WIDTH),
            whole(WIDTH, WIDTH),
            whole(4 * WIDTH, WIDTH),
        ],
        out_specs=[
            each(1, LENGTH, WIDTH + 128),
            each(1, WIDTH, LENGTH),
            each(1, WIDTH, HALF),
            each(1, WIDTH, HALF),
            each(1, HALF, WIDTH),
            whole(8, HALF),
            each(1, HEADS, LENGTH, HALF),
            each(1, 8, 128),
        ],
        compiler_params=pltpu.CompilerParams(vmem_limit_bytes=VMEM_WHOLE),
        cost_estimate=pl.CostEstimate(
            flops=8 * 8 * 512 * 256 * 768, bytes_accessed=25 * 2**20, transcendentals=8 * 2**20
        ),
    )(
        homolog,
        other,
        mask_t,
        mask,
        other_mask,
        row_gain.reshape(1, WIDTH),
        row_in[:, WIDTH : 2 * WIDTH],
        row_in_t,
    )

    after_rows = pl.pallas_call(
        row_kernel,
        out_shape=jax.ShapeDtypeStruct((PEERS, 72, 128), BF16),
        grid=(1,),
        in_specs=[whole(8, 8, 128), whole(WIDTH, WIDTH), whole(8, HALF), here] + [away] * 6,
        out_specs=away,
        scratch_shapes=[
            pltpu.VMEM((SLOTS, HEADS, LENGTH, HALF), BF16),
            pltpu.VMEM((SLOTS, WIDTH, LENGTH), BF16),
            pltpu.VMEM((SLOTS, WIDTH, HALF), BF16),
            pltpu.VMEM((SLOTS, HALF, WIDTH), BF16),
            pltpu.VMEM((HEADS, LENGTH, HALF), F32),
            pltpu.VMEM((HEADS, LENGTH, HALF), BF16),
            pltpu.VMEM((WIDTH, HALF), F32),
            pltpu.VMEM((2, 8 * HALF, 128), F32),
            pltpu.VMEM((PEERS, 72, 128), BF16),
            pltpu.VMEM((LENGTH, WIDTH + 128), BF16),
            pltpu.VMEM((WIDTH, HALF), BF16),
            pltpu.SemaphoreType.DMA((SLOTS, 4)),
            pltpu.SemaphoreType.DMA,
        ],
        compiler_params=pltpu.CompilerParams(vmem_limit_bytes=VMEM_TILE),
        cost_estimate=pl.CostEstimate(
            flops=8 * 8 * 512 * 256 * 512, bytes_accessed=20 * 2**20, transcendentals=0
        ),
    )(safe, row_out, mask_half, tiles, powers, vt, gt, xq, keys, qt)

    columns = lax.all_to_all(after_rows, PLANE, 0, 0, tiled=True)

    finished = pl.pallas_call(
        column_kernel,
        out_shape=jax.ShapeDtypeStruct((4 * LENGTH, WIDTH), BF16),
        grid=(1,),
        in_specs=[here] * 8,
        out_specs=whole(4 * LENGTH, WIDTH),
        scratch_shapes=[
            pltpu.VMEM((PEERS, 9, 8, 128), F32),
            pltpu.VMEM((4, LENGTH, WIDTH), BF16),
            pltpu.VMEM((4, LENGTH, 128), BF16),
            pltpu.VMEM((4, WIDTH, LENGTH), BF16),
            pltpu.VMEM((4, WIDTH, LENGTH), BF16),
            pltpu.VMEM((4, WIDTH, LENGTH), BF16),
            pltpu.VMEM((4, WIDTH, LENGTH), BF16),
            pltpu.VMEM((LENGTH, WIDTH), F32),
            pltpu.VMEM((LENGTH, WIDTH), BF16),
            pltpu.VMEM((2, 4 * LENGTH, 128), F32),
        ],
        compiler_params=params,
        cost_estimate=pl.CostEstimate(
            flops=2 * 8 * 8 * 512 * 256 * 512, bytes_accessed=4 * 2**20, transcendentals=8 * 2**20
        ),
    )(
        columns,
        col_gain.reshape(1, WIDTH),
        col_in[:, WIDTH : 2 * WIDTH],
        col_in_t,
        col_out,
        ff_gain.reshape(1, WIDTH),
        ff_expand,
        ff_shrink,
    )

    back = lax.all_to_all(finished.reshape(128, 16, WIDTH), AXES, 0, 0, tiled=True)
    back = back.reshape(32, 2, 2, 4, 4, WIDTH)
    return jnp.transpose(back, (3, 0, 2, 1, 4, 5)).reshape(4, LENGTH, WIDTH)


def solution(mesh):
    inner = Mesh(mesh.devices.reshape(2, 4, 4, 2, 2), AXES)
    dap = ("z", "x", "yh", "core")
    return jax.shard_map(
        body,
        mesh=inner,
        in_specs=(P(AXES, None, None), P(dap, "grp", None), P(AXES, None)) + (P(),) * 13,
        out_specs=P(AXES, None, None),
        check_vma=False,
    )
```

```python
import functools
import math

import jax
import jax.numpy as jnp
import ml_dtypes
import numpy as np
from jax import lax
from jax.experimental import pallas as pl
from jax.experimental.pallas import tpu as pltpu
from jax.sharding import Mesh, PartitionSpec as P

EPSILON = 1e-05
HEADS = 8
HEAD = 32
WIDTH = 256
LENGTH = 512
HALF = 256
PEERS = 64
LOG2E = math.log2(math.e)
SCALE = HEAD**-0.5 * LOG2E
F32 = jnp.float32
BF16 = jnp.bfloat16
AXES = ("grp", "z", "x", "yh", "core")
PLANE = ("grp", "z", "x", "yh")
VMEM_LIMIT = 40 * 1024 * 1024
SLOTS = 3
VMEM_WHOLE = 60 * 2**20
VMEM_TILE = 58 * 2**20
ROW_BOUND = 40.0
COLUMN_BOUND = 60.0

MASK_TERM = 1e9 * HEAD**0.5


def mask_parts():
    parts = []
    rest = MASK_TERM
    for _ in range(3):
        part = float(np.asarray(rest, ml_dtypes.bfloat16))
        parts.append(part)
        rest -= part
    return parts


def nt(a, b):
    return lax.dot_general(a, b, (((1,), (1,)), ((), ())), preferred_element_type=F32)


def tn(a, b):
    return lax.dot_general(a, b, (((0,), (0,)), ((), ())), preferred_element_type=F32)


def nn(a, b):
    return jnp.dot(a, b, preferred_element_type=F32)


def norm(x, gain):
    average = jnp.mean(x, axis=-1, keepdims=True)
    center = x - average
    spread = jnp.mean(center * center, axis=-1, keepdims=True)
    return (center * lax.rsqrt(spread + EPSILON) * gain).astype(BF16)


def position():
    q = (lax.axis_index("z") * 4 + lax.axis_index("x")) * 2 + lax.axis_index("yh")
    return lax.axis_index("grp"), q, lax.axis_index("core")


def bias_kernel(pair_ref, gain_ref, weight_ref, chain_ref, inter_ref, out_ref):
    grp, q, core = position()
    normed = norm(pair_ref[...].astype(F32), gain_ref[...])
    bias = nt(weight_ref[...], normed)
    chain = chain_ref[...]
    cols = jnp.where(grp == 0, chain[:, :256], chain[:, 256:])
    place = lax.broadcasted_iota(jnp.int32, (8, LENGTH), 1)
    wanted = 16 * q + 8 * core + lax.broadcasted_iota(jnp.int32, (8, LENGTH), 0)
    rows = jnp.sum(jnp.where(place == wanted, chain, 0), axis=1, keepdims=True)
    cross = (rows != cols).astype(F32)
    row = lax.broadcasted_iota(jnp.int32, (8, 8), 0)
    col = lax.broadcasted_iota(jnp.int32, (8, 8), 1)
    inter = jnp.sum(jnp.where(row == col, inter_ref[...], 0.0), axis=1, keepdims=True)
    parts = [
        bias[:, ii * 256 : (ii + 1) * 256] + inter * cross[ii : ii + 1] for ii in range(8)
    ]
    stacked = jnp.stack(parts, axis=0)
    tile = jnp.swapaxes(stacked, 0, 1).reshape(64, 256).astype(BF16)

    def put(p, carry):
        out_ref[p] = tile
        return carry

    lax.fori_loop(0, PEERS, put, 0)


def spread(qt, h, mask_rows):
    at = h % 4
    queries = qt.shape[1]
    pieces = []
    if at:
        pieces.append(jnp.zeros((HEAD * at, queries), BF16))
    pieces.append(qt[h * HEAD : (h + 1) * HEAD])
    if at < 3:
        pieces.append(jnp.zeros((HEAD * (3 - at), queries), BF16))
    pieces.append(mask_rows)
    return jnp.concatenate(pieces, axis=0)


def augment(keys, mask_tile):
    return [jnp.concatenate([keys[:, g * 128 : (g + 1) * 128], mask_tile], axis=1) for g in range(2)]


def score_bound(keys, qt):
    feat = lax.broadcasted_iota(jnp.int32, (WIDTH, 128), 0) // HEAD
    lane = lax.broadcasted_iota(jnp.int32, (WIDTH, 128), 1)
    ones = (feat == lane).astype(F32).astype(BF16)
    feat_t = lax.broadcasted_iota(jnp.int32, (16, WIDTH), 1) // HEAD
    row_t = lax.broadcasted_iota(jnp.int32, (16, WIDTH), 0)
    ones_t = (feat_t == row_t).astype(F32).astype(BF16)
    key_norm = jnp.max(nn(keys * keys, ones))
    query_norm = jnp.max(nn(ones_t, qt * qt))
    return jnp.sqrt(key_norm * 1.02) * jnp.sqrt(query_norm * 1.02) * SCALE


def any_present(tile):
    lane = lax.broadcasted_iota(jnp.int32, tile.shape, 1)
    return jnp.max(jnp.where(lane == 0, tile, -1e30)) > -1.0


def score_powers(keys, mask_tile, qt):
    mask_rows = jnp.ones((128, qt.shape[1]), BF16)
    augmented = augment(keys, mask_tile)
    out = []
    scores = nn(augmented[0], spread(qt, 0, mask_rows))
    for h in range(HEADS):
        later = None
        if h + 1 < HEADS:
            later = nn(augmented[(h + 1) // 4], spread(qt, h + 1, mask_rows))
        out.append(jnp.exp2(scores * SCALE).astype(BF16))
        scores = later
    return out


def blend(vt, h, powers):
    ones_v = jnp.ones((16, LENGTH), BF16)
    blended = nn(jnp.concatenate([vt[h * HEAD : (h + 1) * HEAD], ones_v], axis=0), powers)
    return blended[:HEAD] / blended[HEAD : HEAD + 1]


def attend(parts, between=()):
    mask_rows = jnp.ones((128, HALF), BF16)
    augmented = [augment(keys, tile) for keys, tile, _, _ in parts]
    units = [(part, h) for part in range(len(parts)) for h in range(HEADS)]

    def score(part, h):
        return nn(augmented[part][h // 4], spread(parts[part][3], h, mask_rows))

    out = []
    scores = score(*units[0])
    powers = None
    for at, (part, h) in enumerate(units):
        later = score(*units[at + 1]) if at + 1 < len(units) else None
        now = jnp.exp2(scores * SCALE).astype(BF16)
        if at:
            before = units[at - 1]
            out.append(blend(parts[before[0]][2], before[1], powers))
        powers = now
        scores = later
        for call in between[at * len(between) // len(units) : (at + 1) * len(between) // len(units)]:
            call()
    out.append(blend(parts[units[-1][0]][2], units[-1][1], powers))
    return [
        jnp.concatenate(out[part * HEADS : (part + 1) * HEADS], axis=0)
        for part in range(len(parts))
    ]


def attend_exact(keys, tile, vt, qt, bias_ref):
    key_term = jnp.where(tile[:, :1].astype(F32) < 0.0, -1e9, 0.0)
    feat = lax.broadcasted_iota(jnp.int32, (WIDTH, HALF), 0)

    def head(h, total):
        mine = (feat >= h * HEAD) & (feat < (h + 1) * HEAD)
        queries = jnp.where(mine, qt.astype(F32), 0.0).astype(BF16)
        scores = nn(keys, queries) * HEAD**-0.5
        if bias_ref is not None:
            scores = scores + bias_ref[h]
        scores = scores + key_term
        powers = jnp.exp(scores - jnp.max(scores, axis=0, keepdims=True))
        weights = (powers / jnp.sum(powers, axis=0, keepdims=True)).astype(BF16)
        return jnp.where(mine, nn(vt, weights), total)

    return lax.fori_loop(0, HEADS, head, jnp.zeros((WIDTH, HALF), F32))


def project_kernel(
    own_ref, other_ref, mask_ref, own_mask_ref, other_mask_ref, gain_ref, wk_ref, wt_ref,
    k_ref, vt_ref, qt_ref, gt_ref, xq_ref, mask_out_ref, powers_ref, safe_ref,
):
    step = pl.program_id(0)
    _, _, core = position()
    x = jnp.where(step < 4, own_ref[0].astype(F32), other_ref[0].astype(F32))
    normed = norm(x, gain_ref[...])
    keys = nn(normed, wk_ref[...]).astype(BF16)
    k_ref[0, :, :WIDTH] = keys
    lane = lax.broadcasted_iota(jnp.int32, (8, 128), 1)
    row = lax.broadcasted_iota(jnp.int32, (8, 128), 0)
    consts = mask_parts()
    pick = jnp.zeros((8, 128), F32)
    for at, value in enumerate(consts):
        pick = jnp.where((lane == at) & (row == step), value, pick)
    tile = nn(mask_ref[...] - 1, pick.astype(BF16))
    mask_tile = tile.astype(BF16)
    k_ref[0, :, WIDTH:] = mask_tile
    vt_ref[0] = nt(wt_ref[2 * WIDTH : 3 * WIDTH], normed).astype(BF16)

    def half(a):
        rows = a.reshape(32, 2, 8, WIDTH)
        return jnp.where(core == 0, rows[:, 0], rows[:, 1]).reshape(HALF, WIDTH)

    xq = half(x)
    xq_ref[0] = xq.astype(BF16)
    normed_q = half(normed.astype(F32)).astype(BF16)
    qt = nt(wt_ref[:WIDTH], normed_q).astype(BF16)
    qt_ref[0] = qt
    powers = score_powers(keys, mask_tile, qt)
    for h in range(HEADS):
        powers_ref[0, h] = powers[h]
    bound = score_bound(keys, qt)
    present = any_present(tile)
    safe = (bound <= ROW_BOUND) & present
    safe_ref[0] = jnp.where(safe, 1.0, 0.0) + jnp.zeros((8, 128), F32)
    gt_ref[0] = nt(wt_ref[3 * WIDTH :], normed_q).astype(BF16)

    @pl.when(step == 0)
    def _():
        own = own_mask_ref[...].astype(F32)
        other = other_mask_ref[...].astype(F32)
        first = jnp.where(core == 0, own, other)
        second = jnp.where(core == 0, other, own)
        mask = jnp.concatenate([first, second], axis=0).astype(BF16)
        i = lax.broadcasted_iota(jnp.int32, (LENGTH, HALF), 0)
        l = lax.broadcasted_iota(jnp.int32, (LENGTH, HALF), 1)
        pick = (i == (l // 8) * 16 + core * 8 + l % 8).astype(F32).astype(BF16)
        mask_out_ref[...] = nn(mask, pick).astype(BF16)


def bias_blocks(tile_ref):
    row = lax.broadcasted_iota(jnp.int32, (HALF, HALF), 0)
    col = lax.broadcasted_iota(jnp.int32, (HALF, HALF), 1)
    eye = (row == col).astype(F32).astype(BF16)
    for g in range(2):
        for pair in range(4):
            block = tile_ref[g * 32 : (g + 1) * 32, pair * 16 : (pair + 1) * 16, :]
            block = block.astype(F32).reshape(32, 2, 8, 256)
            for k in range(2):
                rows = block[:, k].reshape(HALF, 256).astype(BF16)
                yield pair * 2 + k, g, nt(eye, rows)


def row_kernel(
    safe_ref, wo_ref, mask_ref, tile_ref, powers_ref, vt_ref, gt_ref, xq_ref, k_ref, qt_ref,
    out_ref, powers_here, vt_here, gt_here, xq_here, bias_ref, factor_ref, o_ref, y_ref, result_ref,
    k_here, qt_here, slot_sem, out_sem,
):
    _, _, core = position()

    def fetch(step):
        slot = lax.rem(step, SLOTS)
        pairs = [(powers_ref, powers_here), (vt_ref, vt_here), (gt_ref, gt_here), (xq_ref, xq_here)]
        return [
            pltpu.make_async_copy(source.at[step], target.at[slot], slot_sem.at[slot, n])
            for n, (source, target) in enumerate(pairs)
        ]

    for step in range(SLOTS):
        for copy in fetch(step):
            copy.start()

    largest = jnp.zeros((8, HALF), F32)
    for h, g, block in bias_blocks(tile_ref):
        block = block * LOG2E
        factor_ref[h, g * 256 : (g + 1) * 256, :] = jnp.exp2(block).astype(BF16)
        size = jnp.abs(block).reshape(32, 8, HALF)
        largest = jnp.maximum(largest, jnp.max(size, axis=0))
    bias_safe = jnp.max(largest) <= ROW_BOUND

    def sequence(step, carry):
        slot = lax.rem(step, SLOTS)
        for copy in fetch(step):
            copy.wait()
        safe = bias_safe & (jnp.max(safe_ref[step]) > 0.5)

        @pl.when(safe)
        def _():
            now = powers_here[slot, 0] * factor_ref[0]
            for h in range(HEADS):
                later = None
                if h + 1 < HEADS:
                    later = powers_here[slot, h + 1] * factor_ref[h + 1]
                o_ref[h * HEAD : (h + 1) * HEAD, :] = blend(vt_here[slot], h, now)
                now = later

        @pl.when(jnp.logical_not(safe))
        def _():
            pltpu.sync_copy(k_ref.at[step], k_here)
            pltpu.sync_copy(qt_ref.at[step], qt_here)
            for h, g, block in bias_blocks(tile_ref):
                bias_ref[h, g * 256 : (g + 1) * 256, :] = block
            o_ref[...] = attend_exact(
                k_here[:, :WIDTH], k_here[:, WIDTH:], vt_here[slot], qt_here[...], bias_ref
            )

        gated = (o_ref[...] * jax.nn.sigmoid(gt_here[slot].astype(F32))).astype(BF16)
        y = xq_here[slot].astype(F32) + tn(gated, wo_ref[...])
        s = lax.rem(step + 4 * core, 8)
        for j in range(2):
            y_ref[j, pl.ds(s, HALF, stride=8), :] = y[:, j * 128 : (j + 1) * 128]

        @pl.when(step + SLOTS < 8)
        def _():
            for copy in fetch(step + SLOTS):
                copy.start()

        return carry

    lax.fori_loop(0, 8, sequence, 0)
    for j in range(2):
        result_ref[:, j * 32 : (j + 1) * 32, :] = y_ref[j].astype(BF16).reshape(PEERS, 32, 128)
        result_ref[j * 32 : (j + 1) * 32, 64:, :] = jnp.broadcast_to(
            mask_ref[:, j * 128 : (j + 1) * 128][None], (32, 8, 128)
        )
    out = pltpu.make_async_copy(result_ref, out_ref, out_sem)
    out.start()
    out.wait()


def column_kernel(
    x_ref, gain_ref, wk_ref, wt_ref, wo_ref, gain2_ref, w1_ref, w2_ref, out_ref,
    x32_ref, keys_ref, tile_ref, vt_ref, qt_ref, gt_ref, o_ref, total_ref, normed_ref, y_ref,
):
    _, q, _ = position()
    x32_ref[...] = x_ref[...].astype(F32).reshape(PEERS, 9, 8, 128)
    absent = (x32_ref[:, 8].reshape(LENGTH, 128) - 1.0).astype(BF16)
    lane = lax.broadcasted_iota(jnp.int32, (128, 128), 1)
    row = lax.broadcasted_iota(jnp.int32, (128, 128), 0)

    def residue_rows(r, first, count):
        halves = [
            x32_ref[first : first + count, 4 * j + r].reshape(count * 8, 128) for j in range(2)
        ]
        return jnp.concatenate(halves, axis=1)

    safe = jnp.bool_(True)
    for r in range(4):
        normed = norm(residue_rows(r, 0, PEERS), gain_ref[...])
        keys = nn(normed, wk_ref[...]).astype(BF16)
        keys_ref[r] = keys
        pick = jnp.zeros((128, 128), F32)
        for at, value in enumerate(mask_parts()):
            pick = jnp.where((lane == at) & (row == 4 * q + r), value, pick)
        tile = nn(absent, pick.astype(BF16))
        tile_ref[r] = tile.astype(BF16)
        vt_ref[r] = nt(wt_ref[2 * WIDTH : 3 * WIDTH], normed).astype(BF16)
        qt = nt(wt_ref[:WIDTH], normed).astype(BF16)
        qt_ref[r] = qt
        gt_ref[r] = nt(wt_ref[3 * WIDTH :], normed).astype(BF16)
        safe = safe & (score_bound(keys, qt) <= COLUMN_BOUND) & any_present(tile)

    def attention(r, between=()):
        parts = [
            (keys_ref[r], tile_ref[r], vt_ref[r], qt_ref[r, :, n * HALF : (n + 1) * HALF])
            for n in range(2)
        ]
        for n, o in enumerate(attend(parts, between)):
            gate(r, n, o)

    def gate(r, n, o):
        cols = slice(n * HALF, (n + 1) * HALF)
        o_ref[r, :, cols] = (o * jax.nn.sigmoid(gt_ref[r, :, cols].astype(F32))).astype(BF16)

    def project_out(r):
        one = residue_rows(r, 0, PEERS) + tn(o_ref[r], wo_ref[...])
        total_ref[...] = one.astype(BF16).astype(F32)

    def normalize():
        normed_ref[...] = norm(total_ref[...], gain2_ref[...])

    def transition(part):
        cols = slice(part * 256, (part + 1) * 256)
        hidden = jnp.maximum(nn(normed_ref[...], w1_ref[:, cols]), 0.0).astype(BF16)
        total_ref[...] += nn(hidden, w2_ref[cols])

    def keep(r):
        for j in range(2):
            y_ref[j, pl.ds(r, LENGTH, stride=4), :] = total_ref[:, j * 128 : (j + 1) * 128]

    def finishing(r):
        blocks = [functools.partial(transition, part) for part in range(4)]
        return [functools.partial(project_out, r), normalize] + blocks + [functools.partial(keep, r)]

    @pl.when(safe)
    def _():
        attention(0)

        def residue(r, carry):
            attention(r, finishing(r - 1))
            return carry

        lax.fori_loop(1, 4, residue, 0)

    @pl.when(jnp.logical_not(safe))
    def _():
        def residue(r, carry):
            for n in range(2):
                queries = qt_ref[r, :, n * HALF : (n + 1) * HALF]
                gate(r, n, attend_exact(keys_ref[r], tile_ref[r], vt_ref[r], queries, None))
            return carry

        lax.fori_loop(0, 4, residue, 0)

        def rest(r, carry):
            for call in finishing(r):
                call()
            return carry

        lax.fori_loop(0, 3, rest, 0)

    for call in finishing(3):
        call()
    for j in range(2):
        out_ref[:, j * 128 : (j + 1) * 128] = y_ref[j].astype(BF16)


def whole(*shape):
    return pl.BlockSpec(shape, lambda i: (0,) * len(shape))


def each(count, *shape):
    return pl.BlockSpec((count,) + shape, lambda i: (i,) + (0,) * len(shape))


def body(
    homolog,
    pair_state,
    mask,
    chain,
    row_gain,
    pair_gain,
    pair_weight,
    interchain,
    row_in,
    row_out,
    col_gain,
    col_in,
    col_out,
    ff_gain,
    ff_expand,
    ff_shrink,
):
    params = pltpu.CompilerParams(vmem_limit_bytes=VMEM_LIMIT)
    here = pl.BlockSpec(memory_space=pltpu.VMEM)
    away = pl.BlockSpec(memory_space=pltpu.HBM)
    swap = [(0, 1), (1, 0)]
    other_mask = lax.ppermute(mask, "core", swap)
    other = lax.ppermute(homolog, "core", swap)

    payload = pl.pallas_call(
        bias_kernel,
        grid=(1,),
        out_shape=jax.ShapeDtypeStruct((PEERS, 64, 256), BF16),
        in_specs=[whole(2048, 128), whole(1, 128), whole(8, 128), whole(1, LENGTH), whole(1, 8)],
        out_specs=whole(PEERS, 64, 256),
        compiler_params=pltpu.CompilerParams(vmem_limit_bytes=VMEM_WHOLE),
    )(
        pair_state.reshape(2048, 128),
        pair_gain.reshape(1, 128),
        pair_weight,
        chain.reshape(1, LENGTH),
        interchain.reshape(1, 8),
    )
    tiles = lax.all_to_all(payload, PLANE, 0, 0, tiled=True)

    row_in_t = row_in.T
    col_in_t = col_in.T
    mask_t = jnp.concatenate([mask, other_mask], axis=0).astype(BF16).T
    keys, vt, qt, gt, xq, mask_half, powers, safe = pl.pallas_call(
        project_kernel,
        grid=(8,),
        out_shape=[
            jax.ShapeDtypeStruct((8, LENGTH, WIDTH + 128), BF16),
            jax.ShapeDtypeStruct((8, WIDTH, LENGTH), BF16),
            jax.ShapeDtypeStruct((8, WIDTH, HALF), BF16),
            jax.ShapeDtypeStruct((8, WIDTH, HALF), BF16),
            jax.ShapeDtypeStruct((8, HALF, WIDTH), BF16),
            jax.ShapeDtypeStruct((8, HALF), BF16),
            jax.ShapeDtypeStruct((8, HEADS, LENGTH, HALF), BF16),
            jax.ShapeDtypeStruct((8, 8, 128), F32),
        ],
        in_specs=[
            pl.BlockSpec((1, LENGTH, WIDTH), lambda i: (jnp.minimum(i, 3), 0, 0)),
            pl.BlockSpec((1, LENGTH, WIDTH), lambda i: (jnp.maximum(i - 4, 0), 0, 0)),
            whole(LENGTH, 8),
            whole(4, LENGTH),
            whole(4, LENGTH),
            whole(1, WIDTH),
            whole(WIDTH, WIDTH),
            whole(4 * WIDTH, WIDTH),
        ],
        out_specs=[
            each(1, LENGTH, WIDTH + 128),
            each(1, WIDTH, LENGTH),
            each(1, WIDTH, HALF),
            each(1, WIDTH, HALF),
            each(1, HALF, WIDTH),
            whole(8, HALF),
            each(1, HEADS, LENGTH, HALF),
            each(1, 8, 128),
        ],
        compiler_params=pltpu.CompilerParams(vmem_limit_bytes=VMEM_WHOLE),
        cost_estimate=pl.CostEstimate(
            flops=8 * 8 * 512 * 256 * 768, bytes_accessed=25 * 2**20, transcendentals=8 * 2**20
        ),
    )(
        homolog,
        other,
        mask_t,
        mask,
        other_mask,
        row_gain.reshape(1, WIDTH),
        row_in[:, WIDTH : 2 * WIDTH],
        row_in_t,
    )

    after_rows = pl.pallas_call(
        row_kernel,
        out_shape=jax.ShapeDtypeStruct((PEERS, 72, 128), BF16),
        grid=(1,),
        in_specs=[whole(8, 8, 128), whole(WIDTH, WIDTH), whole(8, HALF), here] + [away] * 6,
        out_specs=away,
        scratch_shapes=[
            pltpu.VMEM((SLOTS, HEADS, LENGTH, HALF), BF16),
            pltpu.VMEM((SLOTS, WIDTH, LENGTH), BF16),
            pltpu.VMEM((SLOTS, WIDTH, HALF), BF16),
            pltpu.VMEM((SLOTS, HALF, WIDTH), BF16),
            pltpu.VMEM((HEADS, LENGTH, HALF), F32),
            pltpu.VMEM((HEADS, LENGTH, HALF), BF16),
            pltpu.VMEM((WIDTH, HALF), F32),
            pltpu.VMEM((2, 8 * HALF, 128), F32),
            pltpu.VMEM((PEERS, 72, 128), BF16),
            pltpu.VMEM((LENGTH, WIDTH + 128), BF16),
            pltpu.VMEM((WIDTH, HALF), BF16),
            pltpu.SemaphoreType.DMA((SLOTS, 4)),
            pltpu.SemaphoreType.DMA,
        ],
        compiler_params=pltpu.CompilerParams(vmem_limit_bytes=VMEM_TILE),
        cost_estimate=pl.CostEstimate(
            flops=8 * 8 * 512 * 256 * 512, bytes_accessed=20 * 2**20, transcendentals=0
        ),
    )(safe, row_out, mask_half, tiles, powers, vt, gt, xq, keys, qt)

    columns = lax.all_to_all(after_rows, PLANE, 0, 0, tiled=True)

    finished = pl.pallas_call(
        column_kernel,
        out_shape=jax.ShapeDtypeStruct((4 * LENGTH, WIDTH), BF16),
        grid=(1,),
        in_specs=[here] * 8,
        out_specs=whole(4 * LENGTH, WIDTH),
        scratch_shapes=[
            pltpu.VMEM((PEERS, 9, 8, 128), F32),
            pltpu.VMEM((4, LENGTH, WIDTH), BF16),
            pltpu.VMEM((4, LENGTH, 128), BF16),
            pltpu.VMEM((4, WIDTH, LENGTH), BF16),
            pltpu.VMEM((4, WIDTH, LENGTH), BF16),
            pltpu.VMEM((4, WIDTH, LENGTH), BF16),
            pltpu.VMEM((4, WIDTH, LENGTH), BF16),
            pltpu.VMEM((LENGTH, WIDTH), F32),
            pltpu.VMEM((LENGTH, WIDTH), BF16),
            pltpu.VMEM((2, 4 * LENGTH, 128), F32),
        ],
        compiler_params=params,
        cost_estimate=pl.CostEstimate(
            flops=2 * 8 * 8 * 512 * 256 * 512, bytes_accessed=4 * 2**20, transcendentals=8 * 2**20
        ),
    )(
        columns,
        col_gain.reshape(1, WIDTH),
        col_in[:, WIDTH : 2 * WIDTH],
        col_in_t,
        col_out,
        ff_gain.reshape(1, WIDTH),
        ff_expand,
        ff_shrink,
    )

    back = lax.all_to_all(finished.reshape(128, 16, WIDTH), AXES, 0, 0, tiled=True)
    back = back.reshape(32, 2, 2, 4, 4, WIDTH)
    return jnp.transpose(back, (3, 0, 2, 1, 4, 5)).reshape(4, LENGTH, WIDTH)


def solution(mesh):
    inner = Mesh(mesh.devices.reshape(2, 4, 4, 2, 2), AXES)
    dap = ("z", "x", "yh", "core")
    return jax.shard_map(
        body,
        mesh=inner,
        in_specs=(P(AXES, None, None), P(dap, "grp", None), P(AXES, None)) + (P(),) * 13,
        out_specs=P(AXES, None, None),
        check_vma=False,
    )
```

```python
import functools
import math

import jax
import jax.numpy as jnp
import ml_dtypes
import numpy as np
from jax import lax
from jax.experimental import pallas as pl
from jax.experimental.pallas import tpu as pltpu
from jax.sharding import Mesh, PartitionSpec as P

EPSILON = 1e-05
HEADS = 8
HEAD = 32
WIDTH = 256
LENGTH = 512
HALF = 256
PEERS = 64
LOG2E = math.log2(math.e)
SCALE = HEAD**-0.5 * LOG2E
F32 = jnp.float32
BF16 = jnp.bfloat16
AXES = ("grp", "z", "x", "yh", "core")
PLANE = ("grp", "z", "x", "yh")
VMEM_LIMIT = 40 * 1024 * 1024
SLOTS = 3
VMEM_WHOLE = 62 * 2**20
ROW_BOUND = 40.0
COLUMN_BOUND = 60.0

MASK_TERM = 1e9 * HEAD**0.5


def mask_parts():
    parts = []
    rest = MASK_TERM
    for _ in range(3):
        part = float(np.asarray(rest, ml_dtypes.bfloat16))
        parts.append(part)
        rest -= part
    return parts


def nt(a, b):
    return lax.dot_general(a, b, (((1,), (1,)), ((), ())), preferred_element_type=F32)


def tn(a, b):
    return lax.dot_general(a, b, (((0,), (0,)), ((), ())), preferred_element_type=F32)


def nn(a, b):
    return jnp.dot(a, b, preferred_element_type=F32)


def norm(x, gain):
    average = jnp.mean(x, axis=-1, keepdims=True)
    center = x - average
    spread = jnp.mean(center * center, axis=-1, keepdims=True)
    return (center * lax.rsqrt(spread + EPSILON) * gain).astype(BF16)


def position():
    q = (lax.axis_index("z") * 4 + lax.axis_index("x")) * 2 + lax.axis_index("yh")
    return lax.axis_index("grp"), q, lax.axis_index("core")


def bias_kernel(
    pair_ref, gain_ref, weight_ref, chain_ref, inter_ref, out_ref, copies_ref, copy_sem
):
    grp, q, core = position()
    normed = norm(pair_ref[...].astype(F32), gain_ref[...])
    bias = nt(weight_ref[...], normed)
    chain = chain_ref[...]
    cols = jnp.where(grp == 0, chain[:, :256], chain[:, 256:])
    place = lax.broadcasted_iota(jnp.int32, (8, LENGTH), 1)
    wanted = 16 * q + 8 * core + lax.broadcasted_iota(jnp.int32, (8, LENGTH), 0)
    rows = jnp.sum(jnp.where(place == wanted, chain, 0), axis=1, keepdims=True)
    cross = (rows != cols).astype(F32)
    row = lax.broadcasted_iota(jnp.int32, (8, 8), 0)
    col = lax.broadcasted_iota(jnp.int32, (8, 8), 1)
    inter = jnp.sum(jnp.where(row == col, inter_ref[...], 0.0), axis=1, keepdims=True)
    parts = [
        bias[:, ii * 256 : (ii + 1) * 256] + inter * cross[ii : ii + 1] for ii in range(8)
    ]
    stacked = jnp.stack(parts, axis=0)
    tile = jnp.swapaxes(stacked, 0, 1).reshape(64, 256).astype(BF16)

    for n in range(8):
        copies_ref[n] = tile
    sends = [
        pltpu.make_async_copy(copies_ref, out_ref.at[pl.ds(8 * n, 8)], copy_sem.at[n])
        for n in range(8)
    ]
    for send in sends:
        send.start()
    for send in sends:
        send.wait()


def spread(qt, h, mask_rows):
    at = h % 4
    queries = qt.shape[1]
    pieces = []
    if at:
        pieces.append(jnp.zeros((HEAD * at, queries), BF16))
    pieces.append(qt[h * HEAD : (h + 1) * HEAD])
    if at < 3:
        pieces.append(jnp.zeros((HEAD * (3 - at), queries), BF16))
    pieces.append(mask_rows)
    return jnp.concatenate(pieces, axis=0)


def augment(keys, mask_tile):
    return [jnp.concatenate([keys[:, g * 128 : (g + 1) * 128], mask_tile], axis=1) for g in range(2)]


def score_bound(keys, qt):
    feat = lax.broadcasted_iota(jnp.int32, (WIDTH, 128), 0) // HEAD
    lane = lax.broadcasted_iota(jnp.int32, (WIDTH, 128), 1)
    ones = (feat == lane).astype(F32).astype(BF16)
    feat_t = lax.broadcasted_iota(jnp.int32, (16, WIDTH), 1) // HEAD
    row_t = lax.broadcasted_iota(jnp.int32, (16, WIDTH), 0)
    ones_t = (feat_t == row_t).astype(F32).astype(BF16)
    key_norm = jnp.max(nn(keys * keys, ones))
    query_norm = jnp.max(nn(ones_t, qt * qt))
    return jnp.sqrt(key_norm * 1.02) * jnp.sqrt(query_norm * 1.02) * SCALE


def any_present(tile):
    lane = lax.broadcasted_iota(jnp.int32, tile.shape, 1)
    return jnp.max(jnp.where(lane == 0, tile, -1e30)) > -1.0


def score_powers(keys, mask_tile, qt):
    mask_rows = jnp.ones((128, qt.shape[1]), BF16)
    augmented = augment(keys, mask_tile)
    out = []
    scores = nn(augmented[0], spread(qt, 0, mask_rows))
    for h in range(HEADS):
        later = None
        if h + 1 < HEADS:
            later = nn(augmented[(h + 1) // 4], spread(qt, h + 1, mask_rows))
        out.append(jnp.exp2(scores * SCALE).astype(BF16))
        scores = later
    return out


def blend(vt, h, powers):
    ones_v = jnp.ones((16, LENGTH), BF16)
    blended = nn(jnp.concatenate([vt[h * HEAD : (h + 1) * HEAD], ones_v], axis=0), powers)
    return blended[:HEAD] / blended[HEAD : HEAD + 1]


def attend(parts, between=()):
    mask_rows = jnp.ones((128, HALF), BF16)
    augmented = [augment(keys, tile) for keys, tile, _, _ in parts]
    units = [(part, h) for part in range(len(parts)) for h in range(HEADS)]

    def score(part, h):
        return nn(augmented[part][h // 4], spread(parts[part][3], h, mask_rows))

    out = []
    scores = score(*units[0])
    powers = None
    for at, (part, h) in enumerate(units):
        later = score(*units[at + 1]) if at + 1 < len(units) else None
        now = jnp.exp2(scores * SCALE).astype(BF16)
        if at:
            before = units[at - 1]
            out.append(blend(parts[before[0]][2], before[1], powers))
        powers = now
        scores = later
        for call in between[at * len(between) // len(units) : (at + 1) * len(between) // len(units)]:
            call()
    out.append(blend(parts[units[-1][0]][2], units[-1][1], powers))
    return [
        jnp.concatenate(out[part * HEADS : (part + 1) * HEADS], axis=0)
        for part in range(len(parts))
    ]


def attend_exact(keys, tile, vt, qt, bias_ref):
    key_term = jnp.where(tile[:, :1].astype(F32) < 0.0, -1e9, 0.0)
    feat = lax.broadcasted_iota(jnp.int32, (WIDTH, HALF), 0)

    def head(h, total):
        mine = (feat >= h * HEAD) & (feat < (h + 1) * HEAD)
        queries = jnp.where(mine, qt.astype(F32), 0.0).astype(BF16)
        scores = nn(keys, queries) * HEAD**-0.5
        if bias_ref is not None:
            scores = scores + bias_ref[h]
        scores = scores + key_term
        powers = jnp.exp(scores - jnp.max(scores, axis=0, keepdims=True))
        weights = (powers / jnp.sum(powers, axis=0, keepdims=True)).astype(BF16)
        return jnp.where(mine, nn(vt, weights), total)

    return lax.fori_loop(0, HEADS, head, jnp.zeros((WIDTH, HALF), F32))


def project_kernel(
    own_ref, other_ref, mask_ref, own_mask_ref, other_mask_ref, gain_ref, wk_ref, wt_ref,
    k_ref, vt_ref, qt_ref, gt_ref, xq_ref, mask_out_ref, powers_ref, safe_ref,
):
    step = pl.program_id(0)
    _, _, core = position()
    x = jnp.where(step < 4, own_ref[0].astype(F32), other_ref[0].astype(F32))
    normed = norm(x, gain_ref[...])
    keys = nn(normed, wk_ref[...]).astype(BF16)
    k_ref[0, :, :WIDTH] = keys
    lane = lax.broadcasted_iota(jnp.int32, (8, 128), 1)
    row = lax.broadcasted_iota(jnp.int32, (8, 128), 0)
    consts = mask_parts()
    pick = jnp.zeros((8, 128), F32)
    for at, value in enumerate(consts):
        pick = jnp.where((lane == at) & (row == step), value, pick)
    tile = nn(mask_ref[...] - 1, pick.astype(BF16))
    mask_tile = tile.astype(BF16)
    k_ref[0, :, WIDTH:] = mask_tile
    vt_ref[0] = nt(wt_ref[2 * WIDTH : 3 * WIDTH], normed).astype(BF16)

    def half(a):
        rows = a.reshape(32, 2, 8, WIDTH)
        return jnp.where(core == 0, rows[:, 0], rows[:, 1]).reshape(HALF, WIDTH)

    xq = half(x)
    xq_ref[0] = xq.astype(BF16)
    normed_q = half(normed.astype(F32)).astype(BF16)
    qt = nt(wt_ref[:WIDTH], normed_q).astype(BF16)
    qt_ref[0] = qt
    powers = score_powers(keys, mask_tile, qt)
    for h in range(HEADS):
        powers_ref[0, h] = powers[h]
    bound = score_bound(keys, qt)
    present = any_present(tile)
    safe = (bound <= ROW_BOUND) & present
    safe_ref[0] = jnp.where(safe, 1.0, 0.0) + jnp.zeros((8, 128), F32)
    gt_ref[0] = nt(wt_ref[3 * WIDTH :], normed_q).astype(BF16)

    @pl.when(step == 0)
    def _():
        own = own_mask_ref[...].astype(F32)
        other = other_mask_ref[...].astype(F32)
        first = jnp.where(core == 0, own, other)
        second = jnp.where(core == 0, other, own)
        mask = jnp.concatenate([first, second], axis=0).astype(BF16)
        i = lax.broadcasted_iota(jnp.int32, (LENGTH, HALF), 0)
        l = lax.broadcasted_iota(jnp.int32, (LENGTH, HALF), 1)
        pick = (i == (l // 8) * 16 + core * 8 + l % 8).astype(F32).astype(BF16)
        mask_out_ref[...] = nn(mask, pick).astype(BF16)


def bias_blocks(tile_ref):
    row = lax.broadcasted_iota(jnp.int32, (HALF, HALF), 0)
    col = lax.broadcasted_iota(jnp.int32, (HALF, HALF), 1)
    eye = (row == col).astype(F32).astype(BF16)
    for g in range(2):
        for pair in range(4):
            block = tile_ref[g * 32 : (g + 1) * 32, pair * 16 : (pair + 1) * 16, :]
            block = block.astype(F32).reshape(32, 2, 8, 256)
            for k in range(2):
                rows = block[:, k].reshape(HALF, 256).astype(BF16)
                yield pair * 2 + k, g, nt(eye, rows)


def row_kernel(
    safe_ref, wo_ref, mask_ref, tile_ref, powers_ref, vt_ref, gt_ref, xq_ref, k_ref, qt_ref,
    out_ref, powers_here, vt_here, gt_here, xq_here, bias_ref, factor_ref, o_ref, y_ref, result_ref,
    k_here, qt_here, slot_sem, out_sem,
):
    _, _, core = position()

    def fetch(step):
        slot = lax.rem(step, SLOTS)
        pairs = [(powers_ref, powers_here), (vt_ref, vt_here), (gt_ref, gt_here), (xq_ref, xq_here)]
        return [
            pltpu.make_async_copy(source.at[step], target.at[slot], slot_sem.at[slot, n])
            for n, (source, target) in enumerate(pairs)
        ]

    for step in range(SLOTS):
        for copy in fetch(step):
            copy.start()

    largest = jnp.zeros((8, HALF), F32)
    for h, g, block in bias_blocks(tile_ref):
        block = block * LOG2E
        factor_ref[h, g * 256 : (g + 1) * 256, :] = jnp.exp2(block).astype(BF16)
        size = jnp.abs(block).reshape(32, 8, HALF)
        largest = jnp.maximum(largest, jnp.max(size, axis=0))
    bias_safe = jnp.max(largest) <= ROW_BOUND

    def sequence(step, carry):
        slot = lax.rem(step, SLOTS)
        for copy in fetch(step):
            copy.wait()
        safe = bias_safe & (jnp.max(safe_ref[step]) > 0.5)

        @pl.when(safe)
        def _():
            now = powers_here[slot, 0] * factor_ref[0]
            for h in range(HEADS):
                later = None
                if h + 1 < HEADS:
                    later = powers_here[slot, h + 1] * factor_ref[h + 1]
                o_ref[h * HEAD : (h + 1) * HEAD, :] = blend(vt_here[slot], h, now)
                now = later

        @pl.when(jnp.logical_not(safe))
        def _():
            pltpu.sync_copy(k_ref.at[step], k_here)
            pltpu.sync_copy(qt_ref.at[step], qt_here)
            for h, g, block in bias_blocks(tile_ref):
                bias_ref[h, g * 256 : (g + 1) * 256, :] = block
            o_ref[...] = attend_exact(
                k_here[:, :WIDTH], k_here[:, WIDTH:], vt_here[slot], qt_here[...], bias_ref
            )

        gated = (o_ref[...] * jax.nn.sigmoid(gt_here[slot].astype(F32))).astype(BF16)
        y = xq_here[slot].astype(F32) + tn(gated, wo_ref[...])
        s = lax.rem(step + 4 * core, 8)
        for j in range(2):
            y_ref[j, pl.ds(s, HALF, stride=8), :] = y[:, j * 128 : (j + 1) * 128]

        @pl.when(step + SLOTS < 8)
        def _():
            for copy in fetch(step + SLOTS):
                copy.start()

        return carry

    lax.fori_loop(0, 8, sequence, 0)
    for j in range(2):
        result_ref[:, j * 32 : (j + 1) * 32, :] = y_ref[j].astype(BF16).reshape(PEERS, 32, 128)
        result_ref[j * 32 : (j + 1) * 32, 64:, :] = jnp.broadcast_to(
            mask_ref[:, j * 128 : (j + 1) * 128][None], (32, 8, 128)
        )
    out = pltpu.make_async_copy(result_ref, out_ref, out_sem)
    out.start()
    out.wait()


def column_kernel(
    x_ref, gain_ref, wk_ref, wt_ref, wo_ref, gain2_ref, w1_ref, w2_ref, out_ref,
    x32_ref, keys_ref, tile_ref, vt_ref, qt_ref, gt_ref, o_ref, total_ref, normed_ref, y_ref,
):
    _, q, _ = position()
    x32_ref[...] = x_ref[...].astype(F32).reshape(PEERS, 9, 8, 128)
    absent = (x32_ref[:, 8].reshape(LENGTH, 128) - 1.0).astype(BF16)
    lane = lax.broadcasted_iota(jnp.int32, (128, 128), 1)
    row = lax.broadcasted_iota(jnp.int32, (128, 128), 0)

    def residue_rows(r, first, count):
        halves = [
            x32_ref[first : first + count, 4 * j + r].reshape(count * 8, 128) for j in range(2)
        ]
        return jnp.concatenate(halves, axis=1)

    safe = jnp.bool_(True)
    for r in range(4):
        normed = norm(residue_rows(r, 0, PEERS), gain_ref[...])
        keys = nn(normed, wk_ref[...]).astype(BF16)
        keys_ref[r] = keys
        pick = jnp.zeros((128, 128), F32)
        for at, value in enumerate(mask_parts()):
            pick = jnp.where((lane == at) & (row == 4 * q + r), value, pick)
        tile = nn(absent, pick.astype(BF16))
        tile_ref[r] = tile.astype(BF16)
        vt_ref[r] = nt(wt_ref[2 * WIDTH : 3 * WIDTH], normed).astype(BF16)
        qt = nt(wt_ref[:WIDTH], normed).astype(BF16)
        qt_ref[r] = qt
        gt_ref[r] = nt(wt_ref[3 * WIDTH :], normed).astype(BF16)
        safe = safe & (score_bound(keys, qt) <= COLUMN_BOUND) & any_present(tile)

    def attention(r, between=()):
        parts = [
            (keys_ref[r], tile_ref[r], vt_ref[r], qt_ref[r, :, n * HALF : (n + 1) * HALF])
            for n in range(2)
        ]
        for n, o in enumerate(attend(parts, between)):
            gate(r, n, o)

    def gate(r, n, o):
        cols = slice(n * HALF, (n + 1) * HALF)
        o_ref[r, :, cols] = (o * jax.nn.sigmoid(gt_ref[r, :, cols].astype(F32))).astype(BF16)

    def project_out(r):
        one = residue_rows(r, 0, PEERS) + tn(o_ref[r], wo_ref[...])
        total_ref[...] = one.astype(BF16).astype(F32)

    def normalize():
        normed_ref[...] = norm(total_ref[...], gain2_ref[...])

    def transition(part):
        cols = slice(part * 256, (part + 1) * 256)
        hidden = jnp.maximum(nn(normed_ref[...], w1_ref[:, cols]), 0.0).astype(BF16)
        total_ref[...] += nn(hidden, w2_ref[cols])

    def keep(r):
        for j in range(2):
            y_ref[j, pl.ds(r, LENGTH, stride=4), :] = total_ref[:, j * 128 : (j + 1) * 128]

    def finishing(r):
        blocks = [functools.partial(transition, part) for part in range(4)]
        return [functools.partial(project_out, r), normalize] + blocks + [functools.partial(keep, r)]

    @pl.when(safe)
    def _():
        attention(0)

        def residue(r, carry):
            attention(r, finishing(r - 1))
            return carry

        lax.fori_loop(1, 4, residue, 0)

    @pl.when(jnp.logical_not(safe))
    def _():
        def residue(r, carry):
            for n in range(2):
                queries = qt_ref[r, :, n * HALF : (n + 1) * HALF]
                gate(r, n, attend_exact(keys_ref[r], tile_ref[r], vt_ref[r], queries, None))
            return carry

        lax.fori_loop(0, 4, residue, 0)

        def rest(r, carry):
            for call in finishing(r):
                call()
            return carry

        lax.fori_loop(0, 3, rest, 0)

    for call in finishing(3):
        call()
    for j in range(2):
        out_ref[:, j * 128 : (j + 1) * 128] = y_ref[j].astype(BF16)


def whole(*shape):
    return pl.BlockSpec(shape, lambda i: (0,) * len(shape))


def each(count, *shape):
    return pl.BlockSpec((count,) + shape, lambda i: (i,) + (0,) * len(shape))


def body(
    homolog,
    pair_state,
    mask,
    chain,
    row_gain,
    pair_gain,
    pair_weight,
    interchain,
    row_in,
    row_out,
    col_gain,
    col_in,
    col_out,
    ff_gain,
    ff_expand,
    ff_shrink,
):
    params = pltpu.CompilerParams(vmem_limit_bytes=VMEM_LIMIT)
    here = pl.BlockSpec(memory_space=pltpu.VMEM)
    away = pl.BlockSpec(memory_space=pltpu.HBM)
    swap = [(0, 1), (1, 0)]
    other_mask = lax.ppermute(mask, "core", swap)
    other = lax.ppermute(homolog, "core", swap)

    payload = pl.pallas_call(
        bias_kernel,
        grid=(1,),
        out_shape=jax.ShapeDtypeStruct((PEERS, 64, 256), BF16),
        in_specs=[whole(2048, 128), whole(1, 128), whole(8, 128), whole(1, LENGTH), whole(1, 8)],
        out_specs=away,
        scratch_shapes=[pltpu.VMEM((8, 64, 256), BF16), pltpu.SemaphoreType.DMA((8,))],
        compiler_params=pltpu.CompilerParams(vmem_limit_bytes=VMEM_WHOLE),
    )(
        pair_state.reshape(2048, 128),
        pair_gain.reshape(1, 128),
        pair_weight,
        chain.reshape(1, LENGTH),
        interchain.reshape(1, 8),
    )
    tiles = lax.all_to_all(payload, PLANE, 0, 0, tiled=True)

    row_in_t = row_in.T
    col_in_t = col_in.T
    mask_t = jnp.concatenate([mask, other_mask], axis=0).astype(BF16).T
    keys, vt, qt, gt, xq, mask_half, powers, safe = pl.pallas_call(
        project_kernel,
        grid=(8,),
        out_shape=[
            jax.ShapeDtypeStruct((8, LENGTH, WIDTH + 128), BF16),
            jax.ShapeDtypeStruct((8, WIDTH, LENGTH), BF16),
            jax.ShapeDtypeStruct((8, WIDTH, HALF), BF16),
            jax.ShapeDtypeStruct((8, WIDTH, HALF), BF16),
            jax.ShapeDtypeStruct((8, HALF, WIDTH), BF16),
            jax.ShapeDtypeStruct((8, HALF), BF16),
            jax.ShapeDtypeStruct((8, HEADS, LENGTH, HALF), BF16),
            jax.ShapeDtypeStruct((8, 8, 128), F32),
        ],
        in_specs=[
            pl.BlockSpec((1, LENGTH, WIDTH), lambda i: (jnp.minimum(i, 3), 0, 0)),
            pl.BlockSpec((1, LENGTH, WIDTH), lambda i: (jnp.maximum(i - 4, 0), 0, 0)),
            whole(LENGTH, 8),
            whole(4, LENGTH),
            whole(4, LENGTH),
            whole(1, WIDTH),
            whole(WIDTH, WIDTH),
            whole(4 * WIDTH, WIDTH),
        ],
        out_specs=[
            each(1, LENGTH, WIDTH + 128),
            each(1, WIDTH, LENGTH),
            each(1, WIDTH, HALF),
            each(1, WIDTH, HALF),
            each(1, HALF, WIDTH),
            whole(8, HALF),
            each(1, HEADS, LENGTH, HALF),
            each(1, 8, 128),
        ],
        compiler_params=pltpu.CompilerParams(vmem_limit_bytes=VMEM_WHOLE),
        cost_estimate=pl.CostEstimate(
            flops=8 * 8 * 512 * 256 * 768, bytes_accessed=25 * 2**20, transcendentals=8 * 2**20
        ),
    )(
        homolog,
        other,
        mask_t,
        mask,
        other_mask,
        row_gain.reshape(1, WIDTH),
        row_in[:, WIDTH : 2 * WIDTH],
        row_in_t,
    )

    after_rows = pl.pallas_call(
        row_kernel,
        out_shape=jax.ShapeDtypeStruct((PEERS, 72, 128), BF16),
        grid=(1,),
        in_specs=[whole(8, 8, 128), whole(WIDTH, WIDTH), whole(8, HALF), here] + [away] * 6,
        out_specs=away,
        scratch_shapes=[
            pltpu.VMEM((SLOTS, HEADS, LENGTH, HALF), BF16),
            pltpu.VMEM((SLOTS, WIDTH, LENGTH), BF16),
            pltpu.VMEM((SLOTS, WIDTH, HALF), BF16),
            pltpu.VMEM((SLOTS, HALF, WIDTH), BF16),
            pltpu.VMEM((HEADS, LENGTH, HALF), F32),
            pltpu.VMEM((HEADS, LENGTH, HALF), BF16),
            pltpu.VMEM((WIDTH, HALF), F32),
            pltpu.VMEM((2, 8 * HALF, 128), F32),
            pltpu.VMEM((PEERS, 72, 128), BF16),
            pltpu.VMEM((LENGTH, WIDTH + 128), BF16),
            pltpu.VMEM((WIDTH, HALF), BF16),
            pltpu.SemaphoreType.DMA((SLOTS, 4)),
            pltpu.SemaphoreType.DMA,
        ],
        compiler_params=pltpu.CompilerParams(vmem_limit_bytes=VMEM_WHOLE),
        cost_estimate=pl.CostEstimate(
            flops=8 * 8 * 512 * 256 * 512, bytes_accessed=20 * 2**20, transcendentals=0
        ),
    )(safe, row_out, mask_half, tiles, powers, vt, gt, xq, keys, qt)

    columns = lax.all_to_all(after_rows, PLANE, 0, 0, tiled=True)

    finished = pl.pallas_call(
        column_kernel,
        out_shape=jax.ShapeDtypeStruct((4 * LENGTH, WIDTH), BF16),
        grid=(1,),
        in_specs=[here] * 8,
        out_specs=whole(4 * LENGTH, WIDTH),
        scratch_shapes=[
            pltpu.VMEM((PEERS, 9, 8, 128), F32),
            pltpu.VMEM((4, LENGTH, WIDTH), BF16),
            pltpu.VMEM((4, LENGTH, 128), BF16),
            pltpu.VMEM((4, WIDTH, LENGTH), BF16),
            pltpu.VMEM((4, WIDTH, LENGTH), BF16),
            pltpu.VMEM((4, WIDTH, LENGTH), BF16),
            pltpu.VMEM((4, WIDTH, LENGTH), BF16),
            pltpu.VMEM((LENGTH, WIDTH), F32),
            pltpu.VMEM((LENGTH, WIDTH), BF16),
            pltpu.VMEM((2, 4 * LENGTH, 128), F32),
        ],
        compiler_params=params,
        cost_estimate=pl.CostEstimate(
            flops=2 * 8 * 8 * 512 * 256 * 512, bytes_accessed=4 * 2**20, transcendentals=8 * 2**20
        ),
    )(
        columns,
        col_gain.reshape(1, WIDTH),
        col_in[:, WIDTH : 2 * WIDTH],
        col_in_t,
        col_out,
        ff_gain.reshape(1, WIDTH),
        ff_expand,
        ff_shrink,
    )

    back = lax.all_to_all(finished.reshape(128, 16, WIDTH), AXES, 0, 0, tiled=True)
    back = back.reshape(32, 2, 2, 4, 4, WIDTH)
    return jnp.transpose(back, (3, 0, 2, 1, 4, 5)).reshape(4, LENGTH, WIDTH)


def solution(mesh):
    inner = Mesh(mesh.devices.reshape(2, 4, 4, 2, 2), AXES)
    dap = ("z", "x", "yh", "core")
    return jax.shard_map(
        body,
        mesh=inner,
        in_specs=(P(AXES, None, None), P(dap, "grp", None), P(AXES, None)) + (P(),) * 13,
        out_specs=P(AXES, None, None),
        check_vma=False,
    )
```

```python
import functools
import math

import jax
import jax.numpy as jnp
import ml_dtypes
import numpy as np
from jax import lax
from jax.experimental import pallas as pl
from jax.experimental.pallas import tpu as pltpu
from jax.sharding import Mesh, PartitionSpec as P

EPSILON = 1e-05
HEADS = 8
HEAD = 32
WIDTH = 256
LENGTH = 512
HALF = 256
PEERS = 64
ROWS = 2048
LOG2E = math.log2(math.e)
SCALE = HEAD**-0.5 * LOG2E
F32 = jnp.float32
BF16 = jnp.bfloat16
AXES = ("grp", "z", "x", "yh", "core")
PLANE = ("grp", "z", "x", "yh")
VMEM_LIMIT = 40 * 1024 * 1024
SLOTS = 3
VMEM_WHOLE = 62 * 2**20
ROW_BOUND = 40.0
COLUMN_BOUND = 60.0

MASK_TERM = 1e9 * HEAD**0.5


def mask_parts():
    parts = []
    rest = MASK_TERM
    for _ in range(3):
        part = float(np.asarray(rest, ml_dtypes.bfloat16))
        parts.append(part)
        rest -= part
    return parts


def nt(a, b):
    return lax.dot_general(a, b, (((1,), (1,)), ((), ())), preferred_element_type=F32)


def tn(a, b):
    return lax.dot_general(a, b, (((0,), (0,)), ((), ())), preferred_element_type=F32)


def nn(a, b):
    return jnp.dot(a, b, preferred_element_type=F32)


def norm(x, gain):
    average = jnp.mean(x, axis=-1, keepdims=True)
    center = x - average
    spread = jnp.mean(center * center, axis=-1, keepdims=True)
    return (center * lax.rsqrt(spread + EPSILON) * gain).astype(BF16)


def position():
    q = (lax.axis_index("z") * 4 + lax.axis_index("x")) * 2 + lax.axis_index("yh")
    return lax.axis_index("grp"), q, lax.axis_index("core")


def bias_kernel(
    pair_ref, gain_ref, weight_ref, chain_ref, inter_ref, out_ref, copies_ref, copy_sem
):
    grp, q, core = position()
    normed = norm(pair_ref[...].astype(F32), gain_ref[...])
    bias = nt(weight_ref[...], normed)
    chain = chain_ref[...]
    cols = jnp.where(grp == 0, chain[:, :256], chain[:, 256:])
    place = lax.broadcasted_iota(jnp.int32, (8, LENGTH), 1)
    wanted = 16 * q + 8 * core + lax.broadcasted_iota(jnp.int32, (8, LENGTH), 0)
    rows = jnp.sum(jnp.where(place == wanted, chain, 0), axis=1, keepdims=True)
    cross = (rows != cols).astype(F32)
    row = lax.broadcasted_iota(jnp.int32, (8, 8), 0)
    col = lax.broadcasted_iota(jnp.int32, (8, 8), 1)
    inter = jnp.sum(jnp.where(row == col, inter_ref[...], 0.0), axis=1, keepdims=True)
    parts = [
        bias[:, ii * 256 : (ii + 1) * 256] + inter * cross[ii : ii + 1] for ii in range(8)
    ]
    stacked = jnp.stack(parts, axis=0)
    tile = jnp.swapaxes(stacked, 0, 1).reshape(64, 256).astype(BF16)

    for n in range(8):
        copies_ref[n] = tile
    sends = [
        pltpu.make_async_copy(copies_ref, out_ref.at[pl.ds(8 * n, 8)], copy_sem.at[n])
        for n in range(8)
    ]
    for send in sends:
        send.start()
    for send in sends:
        send.wait()


def spread(qt, h, mask_rows):
    at = h % 4
    queries = qt.shape[1]
    pieces = []
    if at:
        pieces.append(jnp.zeros((HEAD * at, queries), BF16))
    pieces.append(qt[h * HEAD : (h + 1) * HEAD])
    if at < 3:
        pieces.append(jnp.zeros((HEAD * (3 - at), queries), BF16))
    pieces.append(mask_rows)
    return jnp.concatenate(pieces, axis=0)


def augment(keys, mask_tile):
    return [jnp.concatenate([keys[:, g * 128 : (g + 1) * 128], mask_tile], axis=1) for g in range(2)]


def score_bound(keys, qt):
    feat = lax.broadcasted_iota(jnp.int32, (WIDTH, 128), 0) // HEAD
    lane = lax.broadcasted_iota(jnp.int32, (WIDTH, 128), 1)
    ones = (feat == lane).astype(F32).astype(BF16)
    feat_t = lax.broadcasted_iota(jnp.int32, (16, WIDTH), 1) // HEAD
    row_t = lax.broadcasted_iota(jnp.int32, (16, WIDTH), 0)
    ones_t = (feat_t == row_t).astype(F32).astype(BF16)
    key_norm = jnp.max(nn(keys * keys, ones))
    query_norm = jnp.max(nn(ones_t, qt * qt))
    return jnp.sqrt(key_norm * 1.02) * jnp.sqrt(query_norm * 1.02) * SCALE


def any_present(tile):
    lane = lax.broadcasted_iota(jnp.int32, tile.shape, 1)
    return jnp.max(jnp.where(lane == 0, tile, -1e30)) > -1.0


def score_powers(keys, mask_tile, qt):
    mask_rows = jnp.ones((128, qt.shape[1]), BF16)
    augmented = augment(keys, mask_tile)
    out = []
    scores = nn(augmented[0], spread(qt, 0, mask_rows))
    for h in range(HEADS):
        later = None
        if h + 1 < HEADS:
            later = nn(augmented[(h + 1) // 4], spread(qt, h + 1, mask_rows))
        out.append(jnp.exp2(scores * SCALE).astype(BF16))
        scores = later
    return out


def blend(vt, h, powers):
    ones_v = jnp.ones((16, LENGTH), BF16)
    blended = nn(jnp.concatenate([vt[h * HEAD : (h + 1) * HEAD], ones_v], axis=0), powers)
    return blended[:HEAD] / blended[HEAD : HEAD + 1]


def attend(parts, between=()):
    mask_rows = jnp.ones((128, HALF), BF16)
    augmented = [augment(keys, tile) for keys, tile, _, _ in parts]
    units = [(part, h) for part in range(len(parts)) for h in range(HEADS)]

    def score(part, h):
        return nn(augmented[part][h // 4], spread(parts[part][3], h, mask_rows))

    out = []
    scores = score(*units[0])
    powers = None
    for at, (part, h) in enumerate(units):
        later = score(*units[at + 1]) if at + 1 < len(units) else None
        now = jnp.exp2(scores * SCALE).astype(BF16)
        if at:
            before = units[at - 1]
            out.append(blend(parts[before[0]][2], before[1], powers))
        powers = now
        scores = later
        for call in between[at * len(between) // len(units) : (at + 1) * len(between) // len(units)]:
            call()
    out.append(blend(parts[units[-1][0]][2], units[-1][1], powers))
    return [
        jnp.concatenate(out[part * HEADS : (part + 1) * HEADS], axis=0)
        for part in range(len(parts))
    ]


def attend_exact(keys, tile, vt, qt, bias_ref):
    key_term = jnp.where(tile[:, :1].astype(F32) < 0.0, -1e9, 0.0)
    feat = lax.broadcasted_iota(jnp.int32, (WIDTH, HALF), 0)

    def head(h, total):
        mine = (feat >= h * HEAD) & (feat < (h + 1) * HEAD)
        queries = jnp.where(mine, qt.astype(F32), 0.0).astype(BF16)
        scores = nn(keys, queries) * HEAD**-0.5
        if bias_ref is not None:
            scores = scores + bias_ref[h]
        scores = scores + key_term
        powers = jnp.exp(scores - jnp.max(scores, axis=0, keepdims=True))
        weights = (powers / jnp.sum(powers, axis=0, keepdims=True)).astype(BF16)
        return jnp.where(mine, nn(vt, weights), total)

    return lax.fori_loop(0, HEADS, head, jnp.zeros((WIDTH, HALF), F32))


def project_kernel(
    own_ref, other_ref, mask_ref, own_mask_ref, other_mask_ref, gain_ref, wk_ref, wt_ref,
    k_ref, vt_ref, qt_ref, gt_ref, xq_ref, mask_out_ref, powers_ref, safe_ref,
):
    step = pl.program_id(0)
    _, _, core = position()
    x = jnp.where(step < 4, own_ref[0].astype(F32), other_ref[0].astype(F32))
    normed = norm(x, gain_ref[...])
    keys = nn(normed, wk_ref[...]).astype(BF16)
    k_ref[0, :, :WIDTH] = keys
    lane = lax.broadcasted_iota(jnp.int32, (8, 128), 1)
    row = lax.broadcasted_iota(jnp.int32, (8, 128), 0)
    consts = mask_parts()
    pick = jnp.zeros((8, 128), F32)
    for at, value in enumerate(consts):
        pick = jnp.where((lane == at) & (row == step), value, pick)
    tile = nn(mask_ref[...] - 1, pick.astype(BF16))
    mask_tile = tile.astype(BF16)
    k_ref[0, :, WIDTH:] = mask_tile
    vt_ref[0] = nt(wt_ref[2 * WIDTH : 3 * WIDTH], normed).astype(BF16)

    def half(a):
        rows = a.reshape(32, 2, 8, WIDTH)
        return jnp.where(core == 0, rows[:, 0], rows[:, 1]).reshape(HALF, WIDTH)

    xq = half(x)
    xq_ref[0] = xq.astype(BF16)
    normed_q = half(normed.astype(F32)).astype(BF16)
    qt = nt(wt_ref[:WIDTH], normed_q).astype(BF16)
    qt_ref[0] = qt
    powers = score_powers(keys, mask_tile, qt)
    for h in range(HEADS):
        powers_ref[0, h] = powers[h]
    bound = score_bound(keys, qt)
    present = any_present(tile)
    safe = (bound <= ROW_BOUND) & present
    safe_ref[0] = jnp.where(safe, 1.0, 0.0) + jnp.zeros((8, 128), F32)
    gt_ref[0] = nt(wt_ref[3 * WIDTH :], normed_q).astype(BF16)

    @pl.when(step == 0)
    def _():
        own = own_mask_ref[...].astype(F32)
        other = other_mask_ref[...].astype(F32)
        first = jnp.where(core == 0, own, other)
        second = jnp.where(core == 0, other, own)
        mask = jnp.concatenate([first, second], axis=0).astype(BF16)
        i = lax.broadcasted_iota(jnp.int32, (LENGTH, HALF), 0)
        l = lax.broadcasted_iota(jnp.int32, (LENGTH, HALF), 1)
        pick = (i == (l // 8) * 16 + core * 8 + l % 8).astype(F32).astype(BF16)
        mask_out_ref[...] = nn(mask, pick).astype(BF16)


def bias_blocks(tile_ref):
    row = lax.broadcasted_iota(jnp.int32, (HALF, HALF), 0)
    col = lax.broadcasted_iota(jnp.int32, (HALF, HALF), 1)
    eye = (row == col).astype(F32).astype(BF16)
    for g in range(2):
        for pair in range(4):
            block = tile_ref[g * 32 : (g + 1) * 32, pair * 16 : (pair + 1) * 16, :]
            block = block.astype(F32).reshape(32, 2, 8, 256)
            for k in range(2):
                rows = block[:, k].reshape(HALF, 256).astype(BF16)
                yield pair * 2 + k, g, nt(eye, rows)


def row_kernel(
    safe_ref, wo_ref, mask_ref, tile_ref, powers_ref, vt_ref, gt_ref, xq_ref, k_ref, qt_ref,
    out_ref, powers_here, vt_here, gt_here, xq_here, bias_ref, factor_ref, o_ref, y_ref, result_ref,
    k_here, qt_here, slot_sem, out_sem,
):
    _, _, core = position()

    def fetch(step):
        slot = lax.rem(step, SLOTS)
        pairs = [(powers_ref, powers_here), (vt_ref, vt_here), (gt_ref, gt_here), (xq_ref, xq_here)]
        return [
            pltpu.make_async_copy(source.at[step], target.at[slot], slot_sem.at[slot, n])
            for n, (source, target) in enumerate(pairs)
        ]

    for step in range(SLOTS):
        for copy in fetch(step):
            copy.start()

    largest = jnp.zeros((8, HALF), F32)
    for h, g, block in bias_blocks(tile_ref):
        block = block * LOG2E
        factor_ref[h, g * 256 : (g + 1) * 256, :] = jnp.exp2(block).astype(BF16)
        size = jnp.abs(block).reshape(32, 8, HALF)
        largest = jnp.maximum(largest, jnp.max(size, axis=0))
    bias_safe = jnp.max(largest) <= ROW_BOUND

    def sequence(step, carry):
        slot = lax.rem(step, SLOTS)
        for copy in fetch(step):
            copy.wait()
        safe = bias_safe & (jnp.max(safe_ref[step]) > 0.5)

        @pl.when(safe)
        def _():
            now = powers_here[slot, 0] * factor_ref[0]
            for h in range(HEADS):
                later = None
                if h + 1 < HEADS:
                    later = powers_here[slot, h + 1] * factor_ref[h + 1]
                o_ref[h * HEAD : (h + 1) * HEAD, :] = blend(vt_here[slot], h, now)
                now = later

        @pl.when(jnp.logical_not(safe))
        def _():
            pltpu.sync_copy(k_ref.at[step], k_here)
            pltpu.sync_copy(qt_ref.at[step], qt_here)
            for h, g, block in bias_blocks(tile_ref):
                bias_ref[h, g * 256 : (g + 1) * 256, :] = block
            o_ref[...] = attend_exact(
                k_here[:, :WIDTH], k_here[:, WIDTH:], vt_here[slot], qt_here[...], bias_ref
            )

        gated = (o_ref[...] * jax.nn.sigmoid(gt_here[slot].astype(F32))).astype(BF16)
        y = xq_here[slot].astype(F32) + tn(gated, wo_ref[...])
        s = lax.rem(step + 4 * core, 8)
        for j in range(2):
            y_ref[j, pl.ds(s, HALF, stride=8), :] = y[:, j * 128 : (j + 1) * 128]

        @pl.when(step + SLOTS < 8)
        def _():
            for copy in fetch(step + SLOTS):
                copy.start()

        return carry

    lax.fori_loop(0, 8, sequence, 0)
    for j in range(2):
        result_ref[:, j * 32 : (j + 1) * 32, :] = y_ref[j, :ROWS].astype(BF16).reshape(PEERS, 32, 128)
        result_ref[j * 32 : (j + 1) * 32, 64:, :] = jnp.broadcast_to(
            mask_ref[:, j * 128 : (j + 1) * 128][None], (32, 8, 128)
        )
    out = pltpu.make_async_copy(result_ref, out_ref, out_sem)
    out.start()
    out.wait()


def column_kernel(
    x_ref, gain_ref, wk_ref, wt_ref, wo_ref, gain2_ref, w1_ref, w2_ref, out_ref,
    x32_ref, keys_ref, tile_ref, vt_ref, qt_ref, gt_ref, o_ref, total_ref, normed_ref, y_ref,
):
    _, q, _ = position()
    x32_ref[...] = x_ref[...].astype(F32).reshape(PEERS, 9, 8, 128)
    absent = (x32_ref[:, 8].reshape(LENGTH, 128) - 1.0).astype(BF16)
    lane = lax.broadcasted_iota(jnp.int32, (128, 128), 1)
    row = lax.broadcasted_iota(jnp.int32, (128, 128), 0)

    def residue_rows(r, first, count):
        halves = [
            x32_ref[first : first + count, 4 * j + r].reshape(count * 8, 128) for j in range(2)
        ]
        return jnp.concatenate(halves, axis=1)

    safe = jnp.bool_(True)
    for r in range(4):
        normed = norm(residue_rows(r, 0, PEERS), gain_ref[...])
        keys = nn(normed, wk_ref[...]).astype(BF16)
        keys_ref[r] = keys
        pick = jnp.zeros((128, 128), F32)
        for at, value in enumerate(mask_parts()):
            pick = jnp.where((lane == at) & (row == 4 * q + r), value, pick)
        tile = nn(absent, pick.astype(BF16))
        tile_ref[r] = tile.astype(BF16)
        vt_ref[r] = nt(wt_ref[2 * WIDTH : 3 * WIDTH], normed).astype(BF16)
        qt = nt(wt_ref[:WIDTH], normed).astype(BF16)
        qt_ref[r] = qt
        gt_ref[r] = nt(wt_ref[3 * WIDTH :], normed).astype(BF16)
        safe = safe & (score_bound(keys, qt) <= COLUMN_BOUND) & any_present(tile)

    def attention(r, between=()):
        parts = [
            (keys_ref[r], tile_ref[r], vt_ref[r], qt_ref[r, :, n * HALF : (n + 1) * HALF])
            for n in range(2)
        ]
        for n, o in enumerate(attend(parts, between)):
            gate(r, n, o)

    def gate(r, n, o):
        cols = slice(n * HALF, (n + 1) * HALF)
        o_ref[r, :, cols] = (o * jax.nn.sigmoid(gt_ref[r, :, cols].astype(F32))).astype(BF16)

    def project_out(r):
        one = residue_rows(r, 0, PEERS) + tn(o_ref[r], wo_ref[...])
        total_ref[...] = one.astype(BF16).astype(F32)

    def normalize():
        normed_ref[...] = norm(total_ref[...], gain2_ref[...])

    def transition(part):
        cols = slice(part * 256, (part + 1) * 256)
        hidden = jnp.maximum(nn(normed_ref[...], w1_ref[:, cols]), 0.0).astype(BF16)
        total_ref[...] += nn(hidden, w2_ref[cols])

    def keep(r):
        for j in range(2):
            y_ref[j, pl.ds(r, LENGTH, stride=4), :] = total_ref[:, j * 128 : (j + 1) * 128]

    def finishing(r):
        blocks = [functools.partial(transition, part) for part in range(4)]
        return [functools.partial(project_out, r), normalize] + blocks + [functools.partial(keep, r)]

    @pl.when(safe)
    def _():
        attention(0)

        def residue(r, carry):
            attention(r, finishing(r - 1))
            return carry

        lax.fori_loop(1, 4, residue, 0)

    @pl.when(jnp.logical_not(safe))
    def _():
        def residue(r, carry):
            for n in range(2):
                queries = qt_ref[r, :, n * HALF : (n + 1) * HALF]
                gate(r, n, attend_exact(keys_ref[r], tile_ref[r], vt_ref[r], queries, None))
            return carry

        lax.fori_loop(0, 4, residue, 0)

        def rest(r, carry):
            for call in finishing(r):
                call()
            return carry

        lax.fori_loop(0, 3, rest, 0)

    for call in finishing(3):
        call()
    for j in range(2):
        out_ref[:, j * 128 : (j + 1) * 128] = y_ref[j, :ROWS].astype(BF16)


def whole(*shape):
    return pl.BlockSpec(shape, lambda i: (0,) * len(shape))


def each(count, *shape):
    return pl.BlockSpec((count,) + shape, lambda i: (i,) + (0,) * len(shape))


def body(
    homolog,
    pair_state,
    mask,
    chain,
    row_gain,
    pair_gain,
    pair_weight,
    interchain,
    row_in,
    row_out,
    col_gain,
    col_in,
    col_out,
    ff_gain,
    ff_expand,
    ff_shrink,
):
    params = pltpu.CompilerParams(vmem_limit_bytes=VMEM_LIMIT)
    here = pl.BlockSpec(memory_space=pltpu.VMEM)
    away = pl.BlockSpec(memory_space=pltpu.HBM)
    swap = [(0, 1), (1, 0)]
    other_mask = lax.ppermute(mask, "core", swap)
    other = lax.ppermute(homolog, "core", swap)

    payload = pl.pallas_call(
        bias_kernel,
        grid=(1,),
        out_shape=jax.ShapeDtypeStruct((PEERS, 64, 256), BF16),
        in_specs=[whole(2048, 128), whole(1, 128), whole(8, 128), whole(1, LENGTH), whole(1, 8)],
        out_specs=away,
        scratch_shapes=[pltpu.VMEM((8, 64, 256), BF16), pltpu.SemaphoreType.DMA((8,))],
        compiler_params=pltpu.CompilerParams(vmem_limit_bytes=VMEM_WHOLE),
    )(
        pair_state.reshape(2048, 128),
        pair_gain.reshape(1, 128),
        pair_weight,
        chain.reshape(1, LENGTH),
        interchain.reshape(1, 8),
    )
    tiles = lax.all_to_all(payload, PLANE, 0, 0, tiled=True)

    row_in_t = row_in.T
    col_in_t = col_in.T
    mask_t = jnp.concatenate([mask, other_mask], axis=0).astype(BF16).T
    keys, vt, qt, gt, xq, mask_half, powers, safe = pl.pallas_call(
        project_kernel,
        grid=(8,),
        out_shape=[
            jax.ShapeDtypeStruct((8, LENGTH, WIDTH + 128), BF16),
            jax.ShapeDtypeStruct((8, WIDTH, LENGTH), BF16),
            jax.ShapeDtypeStruct((8, WIDTH, HALF), BF16),
            jax.ShapeDtypeStruct((8, WIDTH, HALF), BF16),
            jax.ShapeDtypeStruct((8, HALF, WIDTH), BF16),
            jax.ShapeDtypeStruct((8, HALF), BF16),
            jax.ShapeDtypeStruct((8, HEADS, LENGTH, HALF), BF16),
            jax.ShapeDtypeStruct((8, 8, 128), F32),
        ],
        in_specs=[
            pl.BlockSpec((1, LENGTH, WIDTH), lambda i: (jnp.minimum(i, 3), 0, 0)),
            pl.BlockSpec((1, LENGTH, WIDTH), lambda i: (jnp.maximum(i - 4, 0), 0, 0)),
            whole(LENGTH, 8),
            whole(4, LENGTH),
            whole(4, LENGTH),
            whole(1, WIDTH),
            whole(WIDTH, WIDTH),
            whole(4 * WIDTH, WIDTH),
        ],
        out_specs=[
            each(1, LENGTH, WIDTH + 128),
            each(1, WIDTH, LENGTH),
            each(1, WIDTH, HALF),
            each(1, WIDTH, HALF),
            each(1, HALF, WIDTH),
            whole(8, HALF),
            each(1, HEADS, LENGTH, HALF),
            each(1, 8, 128),
        ],
        compiler_params=pltpu.CompilerParams(vmem_limit_bytes=VMEM_WHOLE),
        cost_estimate=pl.CostEstimate(
            flops=8 * 8 * 512 * 256 * 768, bytes_accessed=25 * 2**20, transcendentals=8 * 2**20
        ),
    )(
        homolog,
        other,
        mask_t,
        mask,
        other_mask,
        row_gain.reshape(1, WIDTH),
        row_in[:, WIDTH : 2 * WIDTH],
        row_in_t,
    )

    after_rows = pl.pallas_call(
        row_kernel,
        out_shape=jax.ShapeDtypeStruct((PEERS, 72, 128), BF16),
        grid=(1,),
        in_specs=[whole(8, 8, 128), whole(WIDTH, WIDTH), whole(8, HALF), here] + [away] * 6,
        out_specs=away,
        scratch_shapes=[
            pltpu.VMEM((SLOTS, HEADS, LENGTH, HALF), BF16),
            pltpu.VMEM((SLOTS, WIDTH, LENGTH), BF16),
            pltpu.VMEM((SLOTS, WIDTH, HALF), BF16),
            pltpu.VMEM((SLOTS, HALF, WIDTH), BF16),
            pltpu.VMEM((HEADS, LENGTH, HALF), F32),
            pltpu.VMEM((HEADS, LENGTH, HALF), BF16),
            pltpu.VMEM((WIDTH, HALF), F32),
            pltpu.VMEM((2, ROWS + 8, 128), F32),
            pltpu.VMEM((PEERS, 72, 128), BF16),
            pltpu.VMEM((LENGTH, WIDTH + 128), BF16),
            pltpu.VMEM((WIDTH, HALF), BF16),
            pltpu.SemaphoreType.DMA((SLOTS, 4)),
            pltpu.SemaphoreType.DMA,
        ],
        compiler_params=pltpu.CompilerParams(vmem_limit_bytes=VMEM_WHOLE),
        cost_estimate=pl.CostEstimate(
            flops=8 * 8 * 512 * 256 * 512, bytes_accessed=20 * 2**20, transcendentals=0
        ),
    )(safe, row_out, mask_half, tiles, powers, vt, gt, xq, keys, qt)

    columns = lax.all_to_all(after_rows, PLANE, 0, 0, tiled=True)

    finished = pl.pallas_call(
        column_kernel,
        out_shape=jax.ShapeDtypeStruct((4 * LENGTH, WIDTH), BF16),
        grid=(1,),
        in_specs=[here] * 8,
        out_specs=whole(4 * LENGTH, WIDTH),
        scratch_shapes=[
            pltpu.VMEM((PEERS, 9, 8, 128), F32),
            pltpu.VMEM((4, LENGTH, WIDTH), BF16),
            pltpu.VMEM((4, LENGTH, 128), BF16),
            pltpu.VMEM((4, WIDTH, LENGTH), BF16),
            pltpu.VMEM((4, WIDTH, LENGTH), BF16),
            pltpu.VMEM((4, WIDTH, LENGTH), BF16),
            pltpu.VMEM((4, WIDTH, LENGTH), BF16),
            pltpu.VMEM((LENGTH, WIDTH), F32),
            pltpu.VMEM((LENGTH, WIDTH), BF16),
            pltpu.VMEM((2, ROWS + 8, 128), F32),
        ],
        compiler_params=params,
        cost_estimate=pl.CostEstimate(
            flops=2 * 8 * 8 * 512 * 256 * 512, bytes_accessed=4 * 2**20, transcendentals=8 * 2**20
        ),
    )(
        columns,
        col_gain.reshape(1, WIDTH),
        col_in[:, WIDTH : 2 * WIDTH],
        col_in_t,
        col_out,
        ff_gain.reshape(1, WIDTH),
        ff_expand,
        ff_shrink,
    )

    back = lax.all_to_all(finished.reshape(128, 16, WIDTH), AXES, 0, 0, tiled=True)
    back = back.reshape(32, 2, 2, 4, 4, WIDTH)
    return jnp.transpose(back, (3, 0, 2, 1, 4, 5)).reshape(4, LENGTH, WIDTH)


def solution(mesh):
    inner = Mesh(mesh.devices.reshape(2, 4, 4, 2, 2), AXES)
    dap = ("z", "x", "yh", "core")
    return jax.shard_map(
        body,
        mesh=inner,
        in_specs=(P(AXES, None, None), P(dap, "grp", None), P(AXES, None)) + (P(),) * 13,
        out_specs=P(AXES, None, None),
        check_vma=False,
    )
```

```python
import functools
import math

import jax
import jax.numpy as jnp
import ml_dtypes
import numpy as np
from jax import lax
from jax.experimental import pallas as pl
from jax.experimental.pallas import tpu as pltpu
from jax.sharding import Mesh, PartitionSpec as P

EPSILON = 1e-05
HEADS = 8
HEAD = 32
WIDTH = 256
LENGTH = 512
HALF = 256
PEERS = 64
ROWS = 2048
LOG2E = math.log2(math.e)
SCALE = HEAD**-0.5 * LOG2E
F32 = jnp.float32
BF16 = jnp.bfloat16
AXES = ("grp", "z", "x", "yh", "core")
PLANE = ("grp", "z", "x", "yh")
VMEM_LIMIT = 40 * 1024 * 1024
SLOTS = 3
VMEM_WHOLE = 62 * 2**20
ROW_BOUND = 40.0
COLUMN_BOUND = 60.0

MASK_TERM = 1e9 * HEAD**0.5


def mask_parts():
    parts = []
    rest = MASK_TERM
    for _ in range(3):
        part = float(np.asarray(rest, ml_dtypes.bfloat16))
        parts.append(part)
        rest -= part
    return parts


def nt(a, b):
    return lax.dot_general(a, b, (((1,), (1,)), ((), ())), preferred_element_type=F32)


def tn(a, b):
    return lax.dot_general(a, b, (((0,), (0,)), ((), ())), preferred_element_type=F32)


def nn(a, b):
    return jnp.dot(a, b, preferred_element_type=F32)


def norm(x, gain):
    average = jnp.mean(x, axis=-1, keepdims=True)
    center = x - average
    spread = jnp.mean(center * center, axis=-1, keepdims=True)
    return (center * lax.rsqrt(spread + EPSILON) * gain).astype(BF16)


def position():
    q = (lax.axis_index("z") * 4 + lax.axis_index("x")) * 2 + lax.axis_index("yh")
    return lax.axis_index("grp"), q, lax.axis_index("core")


def bias_kernel(
    pair_ref, gain_ref, weight_ref, chain_ref, inter_ref, out_ref, copies_ref, copy_sem
):
    grp, q, core = position()
    normed = norm(pair_ref[...].astype(F32), gain_ref[...])
    bias = nt(weight_ref[...], normed)
    chain = chain_ref[...]
    cols = jnp.where(grp == 0, chain[:, :256], chain[:, 256:])
    place = lax.broadcasted_iota(jnp.int32, (8, LENGTH), 1)
    wanted = 16 * q + 8 * core + lax.broadcasted_iota(jnp.int32, (8, LENGTH), 0)
    rows = jnp.sum(jnp.where(place == wanted, chain, 0), axis=1, keepdims=True)
    cross = (rows != cols).astype(F32)
    row = lax.broadcasted_iota(jnp.int32, (8, 8), 0)
    col = lax.broadcasted_iota(jnp.int32, (8, 8), 1)
    inter = jnp.sum(jnp.where(row == col, inter_ref[...], 0.0), axis=1, keepdims=True)
    parts = [
        bias[:, ii * 256 : (ii + 1) * 256] + inter * cross[ii : ii + 1] for ii in range(8)
    ]
    stacked = jnp.stack(parts, axis=0)
    tile = jnp.swapaxes(stacked, 0, 1).reshape(64, 256).astype(BF16)

    for n in range(8):
        copies_ref[n] = tile
    sends = [
        pltpu.make_async_copy(copies_ref, out_ref.at[pl.ds(8 * n, 8)], copy_sem.at[n])
        for n in range(8)
    ]
    for send in sends:
        send.start()
    for send in sends:
        send.wait()


def spread(qt, h, mask_rows):
    at = h % 4
    queries = qt.shape[1]
    pieces = []
    if at:
        pieces.append(jnp.zeros((HEAD * at, queries), BF16))
    pieces.append(qt[h * HEAD : (h + 1) * HEAD])
    if at < 3:
        pieces.append(jnp.zeros((HEAD * (3 - at), queries), BF16))
    pieces.append(mask_rows)
    return jnp.concatenate(pieces, axis=0)


def augment(keys, mask_tile):
    return [jnp.concatenate([keys[:, g * 128 : (g + 1) * 128], mask_tile], axis=1) for g in range(2)]


def score_bound(keys, qt):
    feat = lax.broadcasted_iota(jnp.int32, (WIDTH, 128), 0) // HEAD
    lane = lax.broadcasted_iota(jnp.int32, (WIDTH, 128), 1)
    ones = (feat == lane).astype(F32).astype(BF16)
    feat_t = lax.broadcasted_iota(jnp.int32, (16, WIDTH), 1) // HEAD
    row_t = lax.broadcasted_iota(jnp.int32, (16, WIDTH), 0)
    ones_t = (feat_t == row_t).astype(F32).astype(BF16)
    key_norm = most(nn(keys * keys, ones))
    query_norm = most(nn(ones_t, qt * qt))
    return jnp.sqrt(key_norm * 1.02) * jnp.sqrt(query_norm * 1.02) * SCALE


def most(a):
    return jnp.max(jnp.max(a, axis=0, keepdims=True), axis=1, keepdims=True)


def any_present(tile):
    lane = lax.broadcasted_iota(jnp.int32, tile.shape, 1)
    return most(jnp.where(lane == 0, tile, -1e30)) > -1.0


def score_powers(keys, mask_tile, qt):
    mask_rows = jnp.ones((128, qt.shape[1]), BF16)
    augmented = augment(keys, mask_tile)
    out = []
    scores = nn(augmented[0], spread(qt, 0, mask_rows))
    for h in range(HEADS):
        later = None
        if h + 1 < HEADS:
            later = nn(augmented[(h + 1) // 4], spread(qt, h + 1, mask_rows))
        out.append(jnp.exp2(scores * SCALE).astype(BF16))
        scores = later
    return out


def blend(vt, h, powers):
    ones_v = jnp.ones((16, LENGTH), BF16)
    blended = nn(jnp.concatenate([vt[h * HEAD : (h + 1) * HEAD], ones_v], axis=0), powers)
    return blended[:HEAD] / blended[HEAD : HEAD + 1]


def attend(parts, between=()):
    mask_rows = jnp.ones((128, HALF), BF16)
    augmented = [augment(keys, tile) for keys, tile, _, _ in parts]
    units = [(part, h) for part in range(len(parts)) for h in range(HEADS)]

    def score(part, h):
        return nn(augmented[part][h // 4], spread(parts[part][3], h, mask_rows))

    out = []
    scores = score(*units[0])
    powers = None
    for at, (part, h) in enumerate(units):
        later = score(*units[at + 1]) if at + 1 < len(units) else None
        now = jnp.exp2(scores * SCALE).astype(BF16)
        if at:
            before = units[at - 1]
            out.append(blend(parts[before[0]][2], before[1], powers))
        powers = now
        scores = later
        for call in between[at * len(between) // len(units) : (at + 1) * len(between) // len(units)]:
            call()
    out.append(blend(parts[units[-1][0]][2], units[-1][1], powers))
    return [
        jnp.concatenate(out[part * HEADS : (part + 1) * HEADS], axis=0)
        for part in range(len(parts))
    ]


def attend_exact(keys, tile, vt, qt, bias_ref):
    key_term = jnp.where(tile[:, :1].astype(F32) < 0.0, -1e9, 0.0)
    feat = lax.broadcasted_iota(jnp.int32, (WIDTH, HALF), 0)

    def head(h, total):
        mine = (feat >= h * HEAD) & (feat < (h + 1) * HEAD)
        queries = jnp.where(mine, qt.astype(F32), 0.0).astype(BF16)
        scores = nn(keys, queries) * HEAD**-0.5
        if bias_ref is not None:
            scores = scores + bias_ref[h]
        scores = scores + key_term
        powers = jnp.exp(scores - jnp.max(scores, axis=0, keepdims=True))
        weights = (powers / jnp.sum(powers, axis=0, keepdims=True)).astype(BF16)
        return jnp.where(mine, nn(vt, weights), total)

    return lax.fori_loop(0, HEADS, head, jnp.zeros((WIDTH, HALF), F32))


def project_kernel(
    own_ref, other_ref, mask_ref, own_mask_ref, other_mask_ref, gain_ref, wk_ref, wt_ref,
    k_ref, vt_ref, qt_ref, gt_ref, xq_ref, mask_out_ref, powers_ref, safe_ref,
):
    step = pl.program_id(0)
    _, _, core = position()
    x = jnp.where(step < 4, own_ref[0].astype(F32), other_ref[0].astype(F32))
    normed = norm(x, gain_ref[...])
    keys = nn(normed, wk_ref[...]).astype(BF16)
    k_ref[0, :, :WIDTH] = keys
    lane = lax.broadcasted_iota(jnp.int32, (8, 128), 1)
    row = lax.broadcasted_iota(jnp.int32, (8, 128), 0)
    consts = mask_parts()
    pick = jnp.zeros((8, 128), F32)
    for at, value in enumerate(consts):
        pick = jnp.where((lane == at) & (row == step), value, pick)
    tile = nn(mask_ref[...] - 1, pick.astype(BF16))
    mask_tile = tile.astype(BF16)
    k_ref[0, :, WIDTH:] = mask_tile
    vt_ref[0] = nt(wt_ref[2 * WIDTH : 3 * WIDTH], normed).astype(BF16)

    def half(a):
        rows = a.reshape(32, 2, 8, WIDTH)
        return jnp.where(core == 0, rows[:, 0], rows[:, 1]).reshape(HALF, WIDTH)

    xq = half(x)
    xq_ref[0] = xq.astype(BF16)
    normed_q = half(normed.astype(F32)).astype(BF16)
    qt = nt(wt_ref[:WIDTH], normed_q).astype(BF16)
    qt_ref[0] = qt
    powers = score_powers(keys, mask_tile, qt)
    for h in range(HEADS):
        powers_ref[0, h] = powers[h]
    bound = score_bound(keys, qt)
    present = any_present(tile)
    safe = (bound <= ROW_BOUND) & present
    safe_ref[0] = jnp.where(safe, 1.0, 0.0) + jnp.zeros((8, 128), F32)
    gt_ref[0] = nt(wt_ref[3 * WIDTH :], normed_q).astype(BF16)

    @pl.when(step == 0)
    def _():
        own = own_mask_ref[...].astype(F32)
        other = other_mask_ref[...].astype(F32)
        first = jnp.where(core == 0, own, other)
        second = jnp.where(core == 0, other, own)
        mask = jnp.concatenate([first, second], axis=0).astype(BF16)
        i = lax.broadcasted_iota(jnp.int32, (LENGTH, HALF), 0)
        l = lax.broadcasted_iota(jnp.int32, (LENGTH, HALF), 1)
        pick = (i == (l // 8) * 16 + core * 8 + l % 8).astype(F32).astype(BF16)
        mask_out_ref[...] = nn(mask, pick).astype(BF16)


def bias_blocks(tile_ref):
    row = lax.broadcasted_iota(jnp.int32, (HALF, HALF), 0)
    col = lax.broadcasted_iota(jnp.int32, (HALF, HALF), 1)
    eye = (row == col).astype(F32).astype(BF16)
    for g in range(2):
        for pair in range(4):
            block = tile_ref[g * 32 : (g + 1) * 32, pair * 16 : (pair + 1) * 16, :]
            block = block.astype(F32).reshape(32, 2, 8, 256)
            for k in range(2):
                rows = block[:, k].reshape(HALF, 256).astype(BF16)
                yield pair * 2 + k, g, nt(eye, rows)


def row_kernel(
    safe_ref, wo_ref, mask_ref, tile_ref, powers_ref, vt_ref, gt_ref, xq_ref, k_ref, qt_ref,
    out_ref, powers_here, vt_here, gt_here, xq_here, bias_ref, factor_ref, o_ref, y_ref, result_ref,
    k_here, qt_here, slot_sem, out_sem,
):
    _, _, core = position()

    def fetch(step):
        slot = lax.rem(step, SLOTS)
        pairs = [(powers_ref, powers_here), (vt_ref, vt_here), (gt_ref, gt_here), (xq_ref, xq_here)]
        return [
            pltpu.make_async_copy(source.at[step], target.at[slot], slot_sem.at[slot, n])
            for n, (source, target) in enumerate(pairs)
        ]

    for step in range(SLOTS):
        for copy in fetch(step):
            copy.start()

    largest = jnp.zeros((8, HALF), F32)
    for h, g, block in bias_blocks(tile_ref):
        block = block * LOG2E
        factor_ref[h, g * 256 : (g + 1) * 256, :] = jnp.exp2(block).astype(BF16)
        size = jnp.abs(block).reshape(32, 8, HALF)
        largest = jnp.maximum(largest, jnp.max(size, axis=0))
    bias_safe = jnp.max(largest) <= ROW_BOUND

    def sequence(step, carry):
        slot = lax.rem(step, SLOTS)
        for copy in fetch(step):
            copy.wait()
        safe = bias_safe & (jnp.max(safe_ref[step]) > 0.5)

        @pl.when(safe)
        def _():
            now = powers_here[slot, 0] * factor_ref[0]
            for h in range(HEADS):
                later = None
                if h + 1 < HEADS:
                    later = powers_here[slot, h + 1] * factor_ref[h + 1]
                o_ref[h * HEAD : (h + 1) * HEAD, :] = blend(vt_here[slot], h, now)
                now = later

        @pl.when(jnp.logical_not(safe))
        def _():
            pltpu.sync_copy(k_ref.at[step], k_here)
            pltpu.sync_copy(qt_ref.at[step], qt_here)
            for h, g, block in bias_blocks(tile_ref):
                bias_ref[h, g * 256 : (g + 1) * 256, :] = block
            o_ref[...] = attend_exact(
                k_here[:, :WIDTH], k_here[:, WIDTH:], vt_here[slot], qt_here[...], bias_ref
            )

        gated = (o_ref[...] * jax.nn.sigmoid(gt_here[slot].astype(F32))).astype(BF16)
        y = xq_here[slot].astype(F32) + tn(gated, wo_ref[...])
        s = lax.rem(step + 4 * core, 8)
        for j in range(2):
            y_ref[j, pl.ds(s, HALF, stride=8), :] = y[:, j * 128 : (j + 1) * 128]

        @pl.when(step + SLOTS < 8)
        def _():
            for copy in fetch(step + SLOTS):
                copy.start()

        return carry

    lax.fori_loop(0, 8, sequence, 0)
    for j in range(2):
        result_ref[:, j * 32 : (j + 1) * 32, :] = y_ref[j, :ROWS].astype(BF16).reshape(PEERS, 32, 128)
        result_ref[j * 32 : (j + 1) * 32, 64:, :] = jnp.broadcast_to(
            mask_ref[:, j * 128 : (j + 1) * 128][None], (32, 8, 128)
        )
    out = pltpu.make_async_copy(result_ref, out_ref, out_sem)
    out.start()
    out.wait()


def column_kernel(
    x_ref, gain_ref, wk_ref, wt_ref, wo_ref, gain2_ref, w1_ref, w2_ref, out_ref,
    x32_ref, absent_ref, bad_ref, entered_ref, keys_ref, tile_ref, vt_ref, qt_ref, gt_ref, o_ref,
    total_ref, normed_ref, y_ref,
):
    _, q, _ = position()
    x32_ref[...] = x_ref[...].astype(F32).reshape(PEERS, 9, 8, 128)
    absent_ref[...] = (x32_ref[:, 8].reshape(LENGTH, 128) - 1.0).astype(BF16)
    lane = lax.broadcasted_iota(jnp.int32, (128, 128), 1)
    row = lax.broadcasted_iota(jnp.int32, (128, 128), 0)

    def residue_rows(r, first, count):
        halves = [
            x32_ref[first : first + count, 4 * j + r].reshape(count * 8, 128) for j in range(2)
        ]
        return jnp.concatenate(halves, axis=1)

    bad_ref[...] = jnp.zeros((1, 128), F32)

    def enter(r):
        entered_ref[r] = norm(residue_rows(r, 0, PEERS), gain_ref[...])

    def project_keys(r):
        keys_ref[r] = nn(entered_ref[r], wk_ref[...]).astype(BF16)

    def project_others(r, part, ref):
        weight = wt_ref[part * WIDTH : (part + 1) * WIDTH]
        ref[r] = nt(weight, entered_ref[r]).astype(BF16)

    def check(r):
        pick = jnp.zeros((128, 128), F32)
        for at, value in enumerate(mask_parts()):
            pick = jnp.where((lane == at) & (row == 4 * q + r), value, pick)
        tile = nn(absent_ref[...], pick.astype(BF16))
        tile_ref[r] = tile.astype(BF16)
        safe = (score_bound(keys_ref[r], qt_ref[r]) <= COLUMN_BOUND) & any_present(tile)
        bad_ref[...] = jnp.maximum(bad_ref[...], jnp.where(safe, 0.0, 1.0))

    def preparing(r):
        return [
            functools.partial(enter, r),
            functools.partial(project_keys, r),
            functools.partial(project_others, r, 0, qt_ref),
            functools.partial(check, r),
            functools.partial(project_others, r, 2, vt_ref),
            functools.partial(project_others, r, 3, gt_ref),
        ]

    def attention(r, between=()):
        parts = [
            (keys_ref[r], tile_ref[r], vt_ref[r], qt_ref[r, :, n * HALF : (n + 1) * HALF])
            for n in range(2)
        ]
        for n, o in enumerate(attend(parts, between)):
            gate(r, n, o)

    def gate(r, n, o):
        cols = slice(n * HALF, (n + 1) * HALF)
        o_ref[r, :, cols] = (o * jax.nn.sigmoid(gt_ref[r, :, cols].astype(F32))).astype(BF16)

    def project_out(r):
        one = residue_rows(r, 0, PEERS) + tn(o_ref[r], wo_ref[...])
        total_ref[...] = one.astype(BF16).astype(F32)

    def normalize():
        normed_ref[...] = norm(total_ref[...], gain2_ref[...])

    def transition(part):
        cols = slice(part * 256, (part + 1) * 256)
        hidden = jnp.maximum(nn(normed_ref[...], w1_ref[:, cols]), 0.0).astype(BF16)
        total_ref[...] += nn(hidden, w2_ref[cols])

    def keep(r):
        for j in range(2):
            y_ref[j, pl.ds(r, LENGTH, stride=4), :] = total_ref[:, j * 128 : (j + 1) * 128]

    def finishing(r):
        blocks = [functools.partial(transition, part) for part in range(4)]
        return [functools.partial(project_out, r), normalize] + blocks + [functools.partial(keep, r)]

    for call in preparing(0):
        call()
    for r in range(4):
        before = finishing(r - 1) if r else []
        after = preparing(r + 1) if r < 3 else []
        attention(r, before + after)
    for call in finishing(3):
        call()

    @pl.when(jnp.max(bad_ref[...]) > 0.5)
    def _():
        def residue(r, carry):
            for n in range(2):
                queries = qt_ref[r, :, n * HALF : (n + 1) * HALF]
                gate(r, n, attend_exact(keys_ref[r], tile_ref[r], vt_ref[r], queries, None))
            for call in finishing(r):
                call()
            return carry

        lax.fori_loop(0, 4, residue, 0)

    for j in range(2):
        out_ref[:, j * 128 : (j + 1) * 128] = y_ref[j, :ROWS].astype(BF16)


def whole(*shape):
    return pl.BlockSpec(shape, lambda i: (0,) * len(shape))


def each(count, *shape):
    return pl.BlockSpec((count,) + shape, lambda i: (i,) + (0,) * len(shape))


def body(
    homolog,
    pair_state,
    mask,
    chain,
    row_gain,
    pair_gain,
    pair_weight,
    interchain,
    row_in,
    row_out,
    col_gain,
    col_in,
    col_out,
    ff_gain,
    ff_expand,
    ff_shrink,
):
    params = pltpu.CompilerParams(vmem_limit_bytes=VMEM_LIMIT)
    here = pl.BlockSpec(memory_space=pltpu.VMEM)
    away = pl.BlockSpec(memory_space=pltpu.HBM)
    swap = [(0, 1), (1, 0)]
    other_mask = lax.ppermute(mask, "core", swap)
    other = lax.ppermute(homolog, "core", swap)

    payload = pl.pallas_call(
        bias_kernel,
        grid=(1,),
        out_shape=jax.ShapeDtypeStruct((PEERS, 64, 256), BF16),
        in_specs=[whole(2048, 128), whole(1, 128), whole(8, 128), whole(1, LENGTH), whole(1, 8)],
        out_specs=away,
        scratch_shapes=[pltpu.VMEM((8, 64, 256), BF16), pltpu.SemaphoreType.DMA((8,))],
        compiler_params=pltpu.CompilerParams(vmem_limit_bytes=VMEM_WHOLE),
    )(
        pair_state.reshape(2048, 128),
        pair_gain.reshape(1, 128),
        pair_weight,
        chain.reshape(1, LENGTH),
        interchain.reshape(1, 8),
    )
    tiles = lax.all_to_all(payload, PLANE, 0, 0, tiled=True)

    row_in_t = row_in.T
    col_in_t = col_in.T
    mask_t = jnp.concatenate([mask, other_mask], axis=0).astype(BF16).T
    keys, vt, qt, gt, xq, mask_half, powers, safe = pl.pallas_call(
        project_kernel,
        grid=(8,),
        out_shape=[
            jax.ShapeDtypeStruct((8, LENGTH, WIDTH + 128), BF16),
            jax.ShapeDtypeStruct((8, WIDTH, LENGTH), BF16),
            jax.ShapeDtypeStruct((8, WIDTH, HALF), BF16),
            jax.ShapeDtypeStruct((8, WIDTH, HALF), BF16),
            jax.ShapeDtypeStruct((8, HALF, WIDTH), BF16),
            jax.ShapeDtypeStruct((8, HALF), BF16),
            jax.ShapeDtypeStruct((8, HEADS, LENGTH, HALF), BF16),
            jax.ShapeDtypeStruct((8, 8, 128), F32),
        ],
        in_specs=[
            pl.BlockSpec((1, LENGTH, WIDTH), lambda i: (jnp.minimum(i, 3), 0, 0)),
            pl.BlockSpec((1, LENGTH, WIDTH), lambda i: (jnp.maximum(i - 4, 0), 0, 0)),
            whole(LENGTH, 8),
            whole(4, LENGTH),
            whole(4, LENGTH),
            whole(1, WIDTH),
            whole(WIDTH, WIDTH),
            whole(4 * WIDTH, WIDTH),
        ],
        out_specs=[
            each(1, LENGTH, WIDTH + 128),
            each(1, WIDTH, LENGTH),
            each(1, WIDTH, HALF),
            each(1, WIDTH, HALF),
            each(1, HALF, WIDTH),
            whole(8, HALF),
            each(1, HEADS, LENGTH, HALF),
            each(1, 8, 128),
        ],
        compiler_params=pltpu.CompilerParams(vmem_limit_bytes=VMEM_WHOLE),
        cost_estimate=pl.CostEstimate(
            flops=8 * 8 * 512 * 256 * 768, bytes_accessed=25 * 2**20, transcendentals=8 * 2**20
        ),
    )(
        homolog,
        other,
        mask_t,
        mask,
        other_mask,
        row_gain.reshape(1, WIDTH),
        row_in[:, WIDTH : 2 * WIDTH],
        row_in_t,
    )

    after_rows = pl.pallas_call(
        row_kernel,
        out_shape=jax.ShapeDtypeStruct((PEERS, 72, 128), BF16),
        grid=(1,),
        in_specs=[whole(8, 8, 128), whole(WIDTH, WIDTH), whole(8, HALF), here] + [away] * 6,
        out_specs=away,
        scratch_shapes=[
            pltpu.VMEM((SLOTS, HEADS, LENGTH, HALF), BF16),
            pltpu.VMEM((SLOTS, WIDTH, LENGTH), BF16),
            pltpu.VMEM((SLOTS, WIDTH, HALF), BF16),
            pltpu.VMEM((SLOTS, HALF, WIDTH), BF16),
            pltpu.VMEM((HEADS, LENGTH, HALF), F32),
            pltpu.VMEM((HEADS, LENGTH, HALF), BF16),
            pltpu.VMEM((WIDTH, HALF), F32),
            pltpu.VMEM((2, ROWS + 8, 128), F32),
            pltpu.VMEM((PEERS, 72, 128), BF16),
            pltpu.VMEM((LENGTH, WIDTH + 128), BF16),
            pltpu.VMEM((WIDTH, HALF), BF16),
            pltpu.SemaphoreType.DMA((SLOTS, 4)),
            pltpu.SemaphoreType.DMA,
        ],
        compiler_params=pltpu.CompilerParams(vmem_limit_bytes=VMEM_WHOLE),
        cost_estimate=pl.CostEstimate(
            flops=8 * 8 * 512 * 256 * 512, bytes_accessed=20 * 2**20, transcendentals=0
        ),
    )(safe, row_out, mask_half, tiles, powers, vt, gt, xq, keys, qt)

    columns = lax.all_to_all(after_rows, PLANE, 0, 0, tiled=True)

    finished = pl.pallas_call(
        column_kernel,
        out_shape=jax.ShapeDtypeStruct((4 * LENGTH, WIDTH), BF16),
        grid=(1,),
        in_specs=[here] * 8,
        out_specs=whole(4 * LENGTH, WIDTH),
        scratch_shapes=[
            pltpu.VMEM((PEERS, 9, 8, 128), F32),
            pltpu.VMEM((LENGTH, 128), BF16),
            pltpu.VMEM((1, 128), F32),
            pltpu.VMEM((4, LENGTH, WIDTH), BF16),
            pltpu.VMEM((4, LENGTH, WIDTH), BF16),
            pltpu.VMEM((4, LENGTH, 128), BF16),
            pltpu.VMEM((4, WIDTH, LENGTH), BF16),
            pltpu.VMEM((4, WIDTH, LENGTH), BF16),
            pltpu.VMEM((4, WIDTH, LENGTH), BF16),
            pltpu.VMEM((4, WIDTH, LENGTH), BF16),
            pltpu.VMEM((LENGTH, WIDTH), F32),
            pltpu.VMEM((LENGTH, WIDTH), BF16),
            pltpu.VMEM((2, ROWS + 8, 128), F32),
        ],
        compiler_params=params,
        cost_estimate=pl.CostEstimate(
            flops=2 * 8 * 8 * 512 * 256 * 512, bytes_accessed=4 * 2**20, transcendentals=8 * 2**20
        ),
    )(
        columns,
        col_gain.reshape(1, WIDTH),
        col_in[:, WIDTH : 2 * WIDTH],
        col_in_t,
        col_out,
        ff_gain.reshape(1, WIDTH),
        ff_expand,
        ff_shrink,
    )

    back = lax.all_to_all(finished.reshape(128, 16, WIDTH), AXES, 0, 0, tiled=True)
    back = back.reshape(32, 2, 2, 4, 4, WIDTH)
    return jnp.transpose(back, (3, 0, 2, 1, 4, 5)).reshape(4, LENGTH, WIDTH)


def solution(mesh):
    inner = Mesh(mesh.devices.reshape(2, 4, 4, 2, 2), AXES)
    dap = ("z", "x", "yh", "core")
    return jax.shard_map(
        body,
        mesh=inner,
        in_specs=(P(AXES, None, None), P(dap, "grp", None), P(AXES, None)) + (P(),) * 13,
        out_specs=P(AXES, None, None),
        check_vma=False,
    )
```
